32 devices in a mesh: freq: 4 (over x, core), tm: 8 (over z, y).
Axes of the slice: x: 2, y: 2, z: 4, core: 2. Of those that a mesh axis runs over, the one named last changes fastest.
Arguments:
- signal: bfloat16 [2048, 4096], P('tm', 'freq'), may hold values from -48 to 48
- conv_first: bfloat16 [64, 9, 64, 64], P('freq'), may hold values from -0.25 to 0.25
- conv_second: bfloat16 [64, 9, 64, 64], P('freq'), may hold values from -0.25 to 0.25
- shuffle: int32 [64], replicated, may hold values from 0 to 63, each once
- blocks: int32 [2048], P('tm'), may hold values from 0 to 63, never falling along the last dimension, each value on 1 to 64 neighbouring positions
- query_weight: bfloat16 [16, 256, 128], P('freq'), may hold values from -0.25 to 0.25
- key_weight: bfloat16 [16, 256, 128], P('freq'), may hold values from -0.375 to 0.375
- value_weight: bfloat16 [16, 256, 128], P('freq'), may hold values from -0.375 to 0.375
- out_weight: bfloat16 [16, 128, 256], P('freq'), may hold values from -1.796875 to 1.796875
Outputs:
- encoded: bfloat16 [2048, 4096], P('tm', 'freq')
The draws below stay inside these ranges and needn't reach their ends.
All inputs are finite; a program needn't handle non-finite values.
Results may differ from the reference program's by a relative error of at most 0.019.
The reference program's roundings to bfloat16 on the way (of `first`, `shuffled`, `resid`, `weights` and `attended`) count: a program that leaves them out, or rounds other values in their place, can miss the bound.
Values may be sent and summed in bfloat16 or wider, within the bound.
A program may use at most 128 MiB of HBM per device.

```python
import math
import jax
import jax.numpy as jnp
import numpy as np
from jax import lax

G = 64
KS = 9
HEADS = 16
HD = 128
BLK_MOST = 64
TOKENS = 2048
BAND = 256
NBLK = 64


def draw_signal(key, part):
    values = jnp.clip(jax.random.normal(jax.random.fold_in(key, 3), (TOKENS, G * G), jnp.float32), -6.0, 6.0)
    return values.astype(jnp.bfloat16)


def common_base(key):
    return jnp.clip(jax.random.normal(jax.random.fold_in(key, 7), (HEADS, BAND, HD), jnp.float32), -4.0, 4.0)


def draw_query_weight(key, part):
    return (common_base(key) / math.sqrt(BAND)).astype(jnp.bfloat16)


def draw_key_weight(key, part):
    noise = jnp.clip(jax.random.normal(jax.random.fold_in(key, 9), (HEADS, BAND, HD), jnp.float32), -4.0, 4.0)
    mixture = noise
    return (mixture / math.sqrt(BAND)).astype(jnp.bfloat16)


def steps_of(stream_key, shape, cuts, low, top_value):
    gain = 1.0
    for dim, shards_of in cuts:
        steps = jax.random.uniform(jax.random.fold_in(jax.random.fold_in(stream_key, 6), dim), (shards_of,), jnp.float32, low / len(cuts), top_value / len(cuts))
        gain = gain * jnp.repeat(jnp.exp(steps), shape[dim] // shards_of).reshape((-1,) + (1,) * (len(shape) - 1 - dim))
    return gain


def profile(amount, total, bound, slope):
    weights = [(1 << 20) // math.isqrt(rank ** slope) + 1 for rank in range(2, amount + 1)]
    surplus, counts = total - bound - (amount - 1), [1] * (amount - 1)
    while surplus > 0:
        movable = [i for i in range(amount - 1) if counts[i] < bound]
        mass, left = sum([weights[i] for i in movable]), surplus
        for i in movable:
            extra = min(bound - counts[i], max(1, left * weights[i] // mass), surplus)
            counts[i] = counts[i] + extra
            surplus = surplus - extra
    return np.array([bound] + counts)


def ragged_sizes(stream_key, count, total, reach, lean):
    if count == 2:
        one = jax.random.randint(stream_key, (), max(1, total - reach), min(reach, total - 1) + 1)
        return jnp.stack([one, total - one])
    tallies = jnp.asarray(profile(count, total, reach, lean), jnp.int32)
    twos = (count - 1) // 2
    giver, taker = tallies[1:1 + 2 * twos:2], tallies[2:2 + 2 * twos:2]
    slack = jnp.minimum(giver - 1, reach - taker)
    shifted = jax.random.randint(jax.random.fold_in(stream_key, 1), (twos,), 0, 1 << 20) % (slack + 1)
    tallies = tallies.at[1:1 + 2 * twos:2].set(giver - shifted).at[2:2 + 2 * twos:2].set(taker + shifted)
    return tallies[jax.random.permutation(jax.random.fold_in(stream_key, 2), count)]


def bell_draw(key, shape, width, limit, split=(), held_as=jnp.bfloat16):
    entries = jax.random.normal(key, shape, jnp.float32) * width
    if len(split) > 0:
        entries = steps_of(key, shape, split, -0.22, 0.18) * entries
    return jnp.clip(entries, min=-limit, max=limit).astype(held_as)


def setup_inputs(seed: int = 0) -> dict:
    key_of = jax.random.split(jax.random.key(seed), 10)
    signal = draw_signal(jax.random.fold_in(key_of[9], 71), 0)
    conv_first = bell_draw(key_of[1], (G, KS, G, G), (G * KS) ** -0.5, 0.25, ((0, 4),))
    conv_second = bell_draw(key_of[2], (G, KS, G, G), (G * KS) ** -0.5, 0.25, ((0, 4),))
    shuffle = jax.random.permutation(key_of[3], G).astype(jnp.int32)
    blocks = jnp.searchsorted(jnp.cumsum(ragged_sizes(key_of[4], NBLK, TOKENS, BLK_MOST, 1)), jnp.arange(TOKENS), side="right").astype(jnp.int32)
    query_weight = draw_query_weight(jax.random.fold_in(key_of[9], 71), 0)
    key_weight = draw_key_weight(jax.random.fold_in(key_of[9], 71), 0)
    value_weight = bell_draw(key_of[7], (HEADS, BAND, HD), BAND ** -0.5, 0.375, ((0, 4),))
    out_weight = bell_draw(key_of[8], (HEADS, HD, BAND), 0.3, 1.796875, ((0, 4),))
    return dict(signal=signal, conv_first=conv_first, conv_second=conv_second, shuffle=shuffle, blocks=blocks, query_weight=query_weight, key_weight=key_weight, value_weight=value_weight, out_weight=out_weight)


def conv_apply(data, weights, form):
    margin = KS - 1
    length = data.shape[0]
    padded = jnp.concatenate([jnp.zeros((margin,) + data.shape[1:], data.dtype), data], axis=0).astype(jnp.float32)
    result = jnp.zeros((length, data.shape[1], data.shape[2]), jnp.float32)
    for offset in range(KS):
        result = result + jnp.einsum(form, padded[margin - offset:margin - offset + length], weights[:, offset].astype(jnp.float32))
    return result

def head_attend(query_rows, key_rows, value_rows, blocks):
    span = math.gcd(TOKENS, 512)
    scale = 1.0 / math.sqrt(HD)

    def one_block(inputs):
        query_block, query_marks = inputs
        scores = jnp.dot(query_block, key_rows.T, preferred_element_type=jnp.float32) * scale
        seen = blocks[None, :] <= query_marks[:, None]
        masked = jnp.where(seen, scores, jnp.float32(-1e+30))
        peak = lax.optimization_barrier(jnp.max(masked, axis=1, keepdims=True))
        weights = jnp.where(seen, jnp.exp(masked - peak), jnp.float32(0.0))
        total = lax.optimization_barrier(jnp.sum(weights, axis=1, keepdims=True))
        summed = jnp.dot(weights.astype(jnp.bfloat16), value_rows, preferred_element_type=jnp.float32)
        return (summed / total).astype(jnp.bfloat16)
    parts = (query_rows.reshape(TOKENS // span, span, HD), blocks.reshape(TOKENS // span, span))
    return lax.map(one_block, parts).reshape(TOKENS, HD)

def reference(signal, conv_first, conv_second, shuffle, blocks, query_weight, key_weight, value_weight, out_weight):
    grid = signal.reshape(TOKENS, G, G)
    first = jax.nn.silu(conv_apply(grid, conv_first, 'tgi,gio->tgo')).astype(jnp.bfloat16)
    shuffled = first[:, :, shuffle]
    second = conv_apply(shuffled, conv_second, 'tgk,kgo->tko')
    resid = (signal.astype(jnp.float32) + second.reshape(TOKENS, G * G)).astype(jnp.bfloat16)
    bands = resid.reshape(TOKENS, HEADS, BAND).astype(jnp.float32)

    def project(weight):
        return jnp.einsum('thc,hcd->htd', bands, weight.astype(jnp.float32)).astype(jnp.bfloat16)
    queries = project(query_weight)
    keys = project(key_weight)
    values = project(value_weight)

    def per_head(inputs):
        return head_attend(inputs[0], inputs[1], inputs[2], blocks)
    attended = lax.map(per_head, (queries, keys, values))
    added = jnp.einsum('htd,hdc->thc', attended.astype(jnp.float32), out_weight.astype(jnp.float32))
    return (resid.astype(jnp.float32) + added.reshape(TOKENS, G * G)).astype(jnp.bfloat16)
```

```python
import functools
import math

import jax
import jax.numpy as jnp
from jax import lax
from jax.experimental import pallas as pl
from jax.experimental.pallas import tpu as pltpu
from jax.sharding import PartitionSpec as P

MESH = pl.DeviceIdType.MESH
BLOCK_MOST = 64
LANES = 128
F32 = jnp.float32
BF16 = jnp.bfloat16


def ordered_dot(a, b):
    return jnp.dot(a, b, preferred_element_type=F32)


def spread_weights(weights_ref, spread_ref):
    spread_ref[...] = jnp.zeros_like(spread_ref)
    groups, taps, size, _ = weights_ref.shape
    per_band = spread_ref.shape[2] // size
    per_tile = LANES // size
    for group in range(groups):
        place = group % per_band
        tile, slot = place // per_tile, place % per_tile
        block = weights_ref[group]
        parts = [block if i == slot else jnp.zeros_like(block) for i in range(per_tile)]
        spread_ref[
            group // per_band,
            :,
            place * size : (place + 1) * size,
            tile * LANES : (tile + 1) * LANES,
        ] = jnp.concatenate(parts, axis=2)


def layer_kernel(
    freq_count,
    tm_count,
    signal_ref,
    first_ref,
    second_ref,
    source_ref,
    marks_ref,
    wq_ref,
    wk_ref,
    wv_ref,
    wo_ref,
    out_ref,
    padded,
    spread_first,
    spread_second,
    halo,
    first,
    sending,
    arrived,
    shuffled,
    resid,
    pair_out,
    query_out,
    pairs,
    queries,
    marks,
    att_out,
    att_in,
    halo_sem,
    z_send,
    z_recv,
    b_send,
    b_recv,
    kv_send,
    kv_recv,
    q_send,
    q_recv,
    a_send,
    a_recv,
):
    at_freq, at_tm = lax.axis_index("freq"), lax.axis_index("tm")
    count = signal_ref.shape[0]
    heads, band, head_size = wq_ref.shape
    taps = first_ref.shape[1]
    groups = first_ref.shape[0]
    margin = taps - 1
    rows = count + 2 * margin
    splits = tm_count // heads
    part = count // splits

    barrier = pltpu.get_barrier_semaphore()
    for step in range(1, freq_count):
        pl.semaphore_signal(
            barrier,
            inc=1,
            device_id={"freq": lax.rem(at_freq + step, freq_count)},
            device_id_type=MESH,
        )
    for step in range(1, tm_count):
        pl.semaphore_signal(
            barrier,
            inc=1,
            device_id={"tm": lax.rem(at_tm + step, tm_count)},
            device_id_type=MESH,
        )
    spread_weights(first_ref, spread_first)
    for head in range(heads):
        padded[head, 0 : 3 * margin] = jnp.zeros((3 * margin, band), F32)
        padded[head, 3 * margin :] = signal_ref[:, head * band : (head + 1) * band].astype(F32)
    pl.semaphore_wait(barrier, freq_count + tm_count - 2)

    def halo_copy():
        return pltpu.make_async_remote_copy(
            src_ref=signal_ref.at[pl.ds(count - 2 * margin, 2 * margin)],
            dst_ref=halo,
            send_sem=halo_sem.at[0],
            recv_sem=halo_sem.at[1],
            device_id={"tm": lax.rem(at_tm + 1, tm_count)},
            device_id_type=MESH,
        )

    @pl.when(at_tm < tm_count - 1)
    def _():
        halo_copy().start()

    def marks_copy(source, target):
        return pltpu.make_async_remote_copy(
            src_ref=marks_ref,
            dst_ref=marks.at[source],
            send_sem=b_send.at[target],
            recv_sem=b_recv.at[source],
            device_id={"tm": target},
            device_id_type=MESH,
        )

    for step in range(1, tm_count):
        marks_copy(at_tm, lax.rem(at_tm + step, tm_count)).start()
    marks[at_tm] = marks_ref[...]

    @pl.when(at_tm > 0)
    def _():
        halo_copy().wait_recv()
        for head in range(heads):
            padded[head, margin : 3 * margin] = halo[:, head * band : (head + 1) * band].astype(F32)

    def convolve_first(head, carry):
        total = jnp.zeros((rows, band), F32)
        for tap in range(taps):
            window = padded[head, margin - tap : margin - tap + rows].astype(BF16)
            total = total + ordered_dot(window, spread_first[head, tap])
        first[head] = (total / (1.0 + jnp.exp(-total))).astype(BF16)
        return carry

    lax.fori_loop(0, heads, convolve_first, 0)

    columns = arrived.shape[2]
    row_ids = lax.broadcasted_iota(jnp.int32, (heads * band, columns), 0)

    def z_copy(source, target):
        return pltpu.make_async_remote_copy(
            src_ref=sending.at[target],
            dst_ref=arrived.at[source],
            send_sem=z_send.at[target],
            recv_sem=z_recv.at[source],
            device_id={"freq": target},
            device_id_type=MESH,
        )

    def shuffle_for(target):
        picks = jnp.where(row_ids == source_ref[target][0:1, :], 1.0, 0.0).astype(BF16)
        total = ordered_dot(first[0], picks[0:band])
        for head in range(1, heads):
            total = total + ordered_dot(first[head], picks[head * band : (head + 1) * band])
        return total.astype(BF16)

    def shuffle_step(step, carry):
        target = lax.rem(at_freq + step, freq_count)
        sending[target] = shuffle_for(target)
        z_copy(at_freq, target).start()
        return carry

    lax.fori_loop(1, freq_count, shuffle_step, 0)
    arrived[at_freq] = shuffle_for(at_freq)
    spread_weights(second_ref, spread_second)
    for step in range(1, freq_count):
        z_copy(lax.rem(at_freq + step, freq_count), at_freq).wait_recv()

    per_band = groups // heads
    chunk = per_band * groups
    size = band // per_band
    lane_from = lax.broadcasted_iota(jnp.int32, (band, band), 0)
    lane_to = lax.broadcasted_iota(jnp.int32, (band, band), 1)
    wanted = (
        (lane_from % chunk) // groups * size + lane_from // chunk * groups + lane_from % groups
    )
    regroup = jnp.where(wanted == lane_to, 1.0, 0.0).astype(BF16)
    for head in range(heads):
        pieces = [
            arrived[source, :, head * chunk : (head + 1) * chunk] for source in range(freq_count)
        ]
        shuffled[head] = ordered_dot(jnp.concatenate(pieces, axis=1), regroup)

    def pair_copy(source, head, split):
        target = head * splits + split
        return pltpu.make_async_remote_copy(
            src_ref=pair_out.at[head],
            dst_ref=pairs.at[source],
            send_sem=kv_send.at[target],
            recv_sem=kv_recv.at[source],
            device_id={"tm": target},
            device_id_type=MESH,
        )

    def query_copy(source, head, split):
        target = head * splits + split
        return pltpu.make_async_remote_copy(
            src_ref=query_out.at[target],
            dst_ref=queries.at[source],
            send_sem=q_send.at[target],
            recv_sem=q_recv.at[source],
            device_id={"tm": target},
            device_id_type=MESH,
        )

    def project(head):
        total = padded[head, 3 * margin :]
        conv = jnp.zeros((count, band), F32)
        for tap in range(taps):
            window = shuffled[head, 2 * margin - tap : 2 * margin - tap + count].astype(BF16)
            conv = conv + ordered_dot(window, spread_second[head, tap])
        rounded = (total + conv).astype(BF16)
        resid[head] = rounded
        pair_out[head, :, 0:head_size] = ordered_dot(rounded, wk_ref[head]).astype(BF16)
        pair_out[head, :, head_size:] = ordered_dot(rounded, wv_ref[head]).astype(BF16)
        projected = ordered_dot(rounded, wq_ref[head]).astype(BF16)
        for split in range(splits):
            query_out[head * splits + split] = projected[split * part : (split + 1) * part]

    own_head, own_split = at_tm // splits, at_tm % splits

    def project_step(step, carry):
        head = lax.rem(own_head + step, heads)
        project(head)
        for split in range(splits):
            pair_copy(at_tm, head, split).start()
            query_copy(at_tm, head, split).start()
        return carry

    lax.fori_loop(1, heads, project_step, 0)
    project(own_head)
    for split in range(splits):

        @pl.when(own_split != split)
        def _():
            pair_copy(at_tm, own_head, split).start()
            query_copy(at_tm, own_head, split).start()

    pairs[at_tm] = pair_out[own_head]
    queries[at_tm] = query_out[at_tm]

    def att_copy(source, target):
        return pltpu.make_async_remote_copy(
            src_ref=att_out.at[target],
            dst_ref=att_in.at[source],
            send_sem=a_send.at[target],
            recv_sem=a_recv.at[source],
            device_id={"tm": target},
            device_id_type=MESH,
        )

    def await_source(source):
        @pl.when(at_tm != source)
        def _():
            marks_copy(source, at_tm).wait_recv()
            pair_copy(source, own_head, own_split).wait_recv()
            query_copy(source, own_head, own_split).wait_recv()

    factor = math.log2(math.e) / math.sqrt(head_size)
    ahead = -(-BLOCK_MOST // LANES) * LANES
    contract = (((1,), (1,)), ((), ()))
    await_source(0)
    for block in range(tm_count):
        if block + 1 < tm_count:
            await_source(block + 1)
        asked = queries[block]
        near = pairs[block]
        near_marks = marks[block][0:1].astype(F32)
        if block + 1 < tm_count:
            near = jnp.concatenate([near, pairs[block + 1, 0:ahead]], axis=0)
            near_marks = jnp.concatenate(
                [near_marks, marks[block + 1][0:1, 0:ahead].astype(F32)], axis=1
            )
        offset = pl.multiple_of(own_split * part, LANES)
        mine = marks[block, 0:1, pl.ds(offset, part)].astype(F32)
        mine = jnp.transpose(jnp.broadcast_to(mine, (part, part)))[:, 0:1]
        near_scores = lax.dot_general(
            asked, near[:, 0:head_size], contract, preferred_element_type=F32
        )
        near_scores = jnp.where(near_marks <= mine, near_scores, -1e30)
        peak = jnp.max(near_scores, axis=1, keepdims=True)
        if block > 0:
            far = pairs[0:block].reshape(block * count, 2 * head_size)
            far_scores = lax.dot_general(
                asked, far[:, 0:head_size], contract, preferred_element_type=F32
            )
            peak = jnp.maximum(peak, jnp.max(far_scores, axis=1, keepdims=True))
        weights = jnp.exp2((near_scores - peak) * factor)
        total = jnp.sum(weights, axis=1, keepdims=True)
        summed = ordered_dot(weights.astype(BF16), near[:, head_size:])
        if block > 0:
            weights = jnp.exp2((far_scores - peak) * factor)
            total = total + jnp.sum(weights, axis=1, keepdims=True)
            summed = summed + ordered_dot(weights.astype(BF16), far[:, head_size:])
        att_out[block] = (summed / total).astype(BF16)

        @pl.when(at_tm != block)
        def _():
            att_copy(at_tm, block).start()

    att_in[at_tm] = att_out[at_tm]
    for source in range(tm_count):

        @pl.when(at_tm != source)
        def _():
            att_copy(source, at_tm).wait_recv()

        head, split = source // splits, source % splits
        top = split * part
        added = ordered_dot(att_in[source], wo_ref[head])
        out_ref[top : top + part, head * band : (head + 1) * band] = (
            resid[head, top : top + part].astype(F32) + added
        ).astype(BF16)

    @pl.when(at_tm < tm_count - 1)
    def _():
        halo_copy().wait_send()

    for step in range(1, freq_count):
        z_copy(at_freq, lax.rem(at_freq + step, freq_count)).wait_send()
    for step in range(1, tm_count):
        target = lax.rem(at_tm + step, tm_count)
        marks_copy(at_tm, target).wait_send()
        pair_copy(at_tm, target // splits, target % splits).wait_send()
        query_copy(at_tm, target // splits, target % splits).wait_send()
        att_copy(at_tm, target).wait_send()


def per_device_fused(
    signal,
    conv_first,
    conv_second,
    shuffle,
    blocks,
    query_weight,
    key_weight,
    value_weight,
    out_weight,
):
    freq_count, tm_count = lax.axis_size("freq"), lax.axis_size("tm")
    count, width = signal.shape
    groups, taps, size, _ = conv_first.shape
    heads, band, head_size = query_weight.shape
    margin = taps - 1
    rows = count + 2 * margin
    part = count * heads // tm_count
    columns = groups * groups
    source = shuffle.reshape(freq_count, groups, 1) + size * jnp.arange(groups, dtype=jnp.int32)
    source = jnp.broadcast_to(
        source.reshape(freq_count, 1, columns), (freq_count, 8, columns)
    )
    marks = jnp.broadcast_to(blocks[None, :], (8, count))
    vmem = pl.BlockSpec(memory_space=pltpu.VMEM)
    dma = pltpu.SemaphoreType.DMA
    return pl.pallas_call(
        functools.partial(layer_kernel, freq_count, tm_count),
        out_shape=jax.ShapeDtypeStruct((count, width), BF16),
        in_specs=[vmem] * 9,
        out_specs=vmem,
        scratch_shapes=[
            pltpu.VMEM((heads, rows + margin, band), F32),
            pltpu.VMEM((heads, taps, band, band), BF16),
            pltpu.VMEM((heads, taps, band, band), BF16),
            pltpu.VMEM((2 * margin, width), BF16),
            pltpu.VMEM((heads, rows, band), BF16),
            pltpu.VMEM((freq_count, rows, columns), BF16),
            pltpu.VMEM((freq_count, rows, columns), BF16),
            pltpu.VMEM((heads, rows, band), F32),
            pltpu.VMEM((heads, count, band), BF16),
            pltpu.VMEM((heads, count, 2 * head_size), BF16),
            pltpu.VMEM((tm_count, part, head_size), BF16),
            pltpu.VMEM((tm_count, count, 2 * head_size), BF16),
            pltpu.VMEM((tm_count, part, head_size), BF16),
            pltpu.VMEM((tm_count, 8, count), jnp.int32),
            pltpu.VMEM((tm_count, part, head_size), BF16),
            pltpu.VMEM((tm_count, part, head_size), BF16),
            dma((2,)),
            dma((freq_count,)),
            dma((freq_count,)),
        ]
        + [dma((tm_count,))] * 8,
        compiler_params=pltpu.CompilerParams(
            collective_id=0, has_side_effects=True, vmem_limit_bytes=56 * 1024 * 1024
        ),
        cost_estimate=pl.CostEstimate(
            flops=10**10, bytes_accessed=8 * 10**6, transcendentals=2 * 10**6
        ),
    )(
        signal,
        conv_first,
        conv_second,
        source,
        marks,
        query_weight,
        key_weight,
        value_weight,
        out_weight,
    )


def fits_fused(signal, conv_first, query_weight):
    tm_count = lax.axis_size("tm")
    count = signal.shape[0]
    groups, taps, size, _ = conv_first.shape
    heads, band, head_size = query_weight.shape
    return (
        tm_count % heads == 0
        and (count * heads) % (LANES * tm_count) == 0
        and (groups * groups) % LANES == 0
        and groups % heads == 0
        and heads * band == signal.shape[1]
        and (taps - 1) % 8 == 0
        and LANES % size == 0
        and band % LANES == 0
        and head_size % LANES == 0
        and size % 16 == 0
    )


def passed_along(block, axis, distance):
    devices = range(lax.axis_size(axis))
    route = [(i - distance, i) for i in devices if i - distance in devices]
    return lax.ppermute(block, axis, route)


def conv_local(padded, weights, length, form):
    margin = weights.shape[1] - 1
    result = None
    for offset in range(weights.shape[1]):
        term = jnp.einsum(
            form,
            padded[margin - offset : margin - offset + length],
            weights[:, offset],
            preferred_element_type=jnp.float32,
        )
        result = term if result is None else result + term
    return result


def split_range(count, width):
    return [(offset, min(offset + width, count)) for offset in range(0, count, width)]


def update_tile(state, query_part, query_marks, key_part, value_part, key_marks):
    peak, total, summed = state
    scale = 1.0 / math.sqrt(query_part.shape[2])
    scores = (
        jnp.einsum("qhd,khd->hqk", query_part, key_part, preferred_element_type=jnp.float32) * scale
    )
    seen = key_marks[None, None, :] <= query_marks[None, :, None]
    masked = jnp.where(seen, scores, jnp.float32(-1e30))
    new_peak = jnp.maximum(peak, jnp.max(masked, axis=2))
    weights = jnp.where(seen, jnp.exp(masked - new_peak[:, :, None]), jnp.float32(0.0))
    factor = jnp.exp(peak - new_peak)
    total = total * factor + jnp.sum(weights, axis=2)
    summed = summed * factor[:, :, None] + jnp.einsum(
        "hqk,khd->hqd", weights.astype(jnp.bfloat16), value_part, preferred_element_type=jnp.float32
    )
    return (new_peak, total, summed)


def unchanged(state, *others):
    return state


def make_fold(queries, query_marks):
    count = queries.shape[0]
    query_cuts = split_range(count, max(1, count // 2))

    def fold(carry, piece, start):
        key_rows, value_rows, key_marks = piece
        key_cuts = split_range(key_rows.shape[0], max(1, count // 2))
        peak, total, summed = carry
        results = []
        for top_row, end_row in query_cuts:
            state = (
                peak[:, top_row:end_row],
                total[:, top_row:end_row],
                summed[:, top_row:end_row],
            )
            for key_top, key_end in key_cuts:
                needed = jnp.min(key_marks[key_top:key_end]) <= jnp.max(
                    query_marks[top_row:end_row]
                )
                state = lax.cond(
                    needed,
                    update_tile,
                    unchanged,
                    state,
                    queries[top_row:end_row],
                    query_marks[top_row:end_row],
                    key_rows[key_top:key_end],
                    value_rows[key_top:key_end],
                    key_marks[key_top:key_end],
                )
            results.append(state)
        return tuple(
            (jnp.concatenate([entry[member] for entry in results], axis=1) for member in range(3))
        )

    return fold


def start_state(heads_here, count, head_size):
    return (
        jnp.full((heads_here, count), -1e30, jnp.float32),
        jnp.zeros((heads_here, count), jnp.float32),
        jnp.zeros((heads_here, count, head_size), jnp.float32),
    )


def finish(state):
    peak, total, summed = state
    return jnp.transpose(summed / total[:, :, None], (1, 0, 2)).astype(jnp.bfloat16)


def per_device_plain(
    signal,
    conv_first,
    conv_second,
    shuffle,
    blocks,
    query_weight,
    key_weight,
    value_weight,
    out_weight,
):
    count, width = signal.shape
    groups_here = conv_first.shape[0]
    group_size = conv_first.shape[2]
    margin = conv_first.shape[1] - 1
    local = signal.reshape(count, groups_here, group_size)
    selector = (shuffle[None, :] == jnp.arange(group_size, dtype=jnp.int32)[:, None]).astype(
        jnp.bfloat16
    )
    before = passed_along(local[count - 2 * margin :], "tm", 1)
    padded = jnp.concatenate([before, local], axis=0)
    first = jax.nn.silu(conv_local(padded, conv_first, count + margin, "tgi,gio->tgo")).astype(
        jnp.bfloat16
    )
    permuted = jnp.einsum(
        "tgj,jk->tgk", first, selector, preferred_element_type=jnp.float32
    ).astype(jnp.bfloat16)
    shuffled = lax.all_to_all(permuted, "freq", split_axis=2, concat_axis=1, tiled=True)
    second = conv_local(shuffled, conv_second, count, "tgk,kgo->tko")
    resid = (signal.astype(jnp.float32) + second.reshape(count, width)).astype(jnp.bfloat16)
    heads_here, band, head_size = query_weight.shape
    bands = resid.reshape(count, heads_here, band)
    queries = jnp.einsum(
        "thc,hcd->thd", bands, query_weight, preferred_element_type=jnp.float32
    ).astype(jnp.bfloat16)
    keys = jnp.einsum("thc,hcd->thd", bands, key_weight, preferred_element_type=jnp.float32).astype(
        jnp.bfloat16
    )
    values = jnp.einsum(
        "thc,hcd->thd", bands, value_weight, preferred_element_type=jnp.float32
    ).astype(jnp.bfloat16)
    initial = start_state(heads_here, count, head_size)
    fold = make_fold(queries, blocks)
    state = fold(
        initial,
        (
            lax.all_gather(keys, "tm", axis=0, tiled=True),
            lax.all_gather(values, "tm", axis=0, tiled=True),
            lax.all_gather(blocks, "tm", axis=0, tiled=True),
        ),
        jnp.int32(0),
    )
    attended = finish(state)
    added = jnp.einsum("thd,hdc->thc", attended, out_weight, preferred_element_type=jnp.float32)
    return (resid.astype(jnp.float32) + added.reshape(count, width)).astype(jnp.bfloat16)


def per_device(*args):
    if fits_fused(args[0], args[1], args[5]):
        return per_device_fused(*args)
    return per_device_plain(*args)


def solution(mesh):
    in_specs = (
        P("tm", "freq"),
        P("freq", None, None, None),
        P("freq", None, None, None),
        P(),
        P("tm"),
        P("freq", None, None),
        P("freq", None, None),
        P("freq", None, None),
        P("freq", None, None),
    )
    out_specs = P("tm", "freq")
    return jax.shard_map(
        per_device, mesh=mesh, in_specs=in_specs, out_specs=out_specs, check_vma=False
    )
```

```python
import functools
import math

import jax
import jax.numpy as jnp
from jax import lax
from jax.experimental import pallas as pl
from jax.experimental.pallas import tpu as pltpu
from jax.sharding import PartitionSpec as P

MESH = pl.DeviceIdType.MESH
BLOCK_MOST = 64
LANES = 128
F32 = jnp.float32
BF16 = jnp.bfloat16


def ordered_dot(a, b):
    return jnp.dot(a, b, preferred_element_type=F32)


def spread_weights(weights_ref, spread_ref):
    spread_ref[...] = jnp.zeros_like(spread_ref)
    groups, taps, size, _ = weights_ref.shape
    per_band = spread_ref.shape[2] // size
    per_tile = LANES // size
    for group in range(groups):
        place = group % per_band
        tile, slot = place // per_tile, place % per_tile
        block = weights_ref[group]
        parts = [block if i == slot else jnp.zeros_like(block) for i in range(per_tile)]
        spread_ref[
            group // per_band,
            :,
            place * size : (place + 1) * size,
            tile * LANES : (tile + 1) * LANES,
        ] = jnp.concatenate(parts, axis=2)


def layer_kernel(
    freq_count,
    tm_count,
    signal_ref,
    first_ref,
    shuffle_ref,
    blocks_ref,
    second_hbm,
    wq_hbm,
    wk_hbm,
    wv_hbm,
    wo_hbm,
    out_ref,
    second_ref,
    wq_ref,
    wk_ref,
    wv_ref,
    wo_ref,
    source_ref,
    marks_ref,
    padded,
    spread_first,
    spread_second,
    halo,
    first,
    sending,
    arrived,
    shuffled,
    resid,
    pair_out,
    query_out,
    pairs,
    queries,
    marks,
    att_out,
    att_in,
    halo_sem,
    z_send,
    z_recv,
    b_send,
    b_recv,
    kv_send,
    kv_recv,
    q_send,
    q_recv,
    a_send,
    a_recv,
    forward_send,
    load_sem,
):
    at_freq, at_tm = lax.axis_index("freq"), lax.axis_index("tm")
    count = signal_ref.shape[0]
    heads, band, head_size = wq_ref.shape
    taps = first_ref.shape[1]
    groups = first_ref.shape[0]
    margin = taps - 1
    rows = count + 2 * margin
    splits = tm_count // heads
    part = count // splits

    barrier = pltpu.get_barrier_semaphore()
    for step in range(1, freq_count):
        pl.semaphore_signal(
            barrier,
            inc=1,
            device_id={"freq": lax.rem(at_freq + step, freq_count)},
            device_id_type=MESH,
        )
    for step in range(1, tm_count):
        pl.semaphore_signal(
            barrier,
            inc=1,
            device_id={"tm": lax.rem(at_tm + step, tm_count)},
            device_id_type=MESH,
        )
    loads = [
        pltpu.make_async_copy(whole, local, load_sem.at[i])
        for i, (whole, local) in enumerate(
            (
                (second_hbm, second_ref),
                (wq_hbm, wq_ref),
                (wk_hbm, wk_ref),
                (wv_hbm, wv_ref),
                (wo_hbm, wo_ref),
            )
        )
    ]
    for load in loads:
        load.start()
    marks_ref[...] = jnp.broadcast_to(blocks_ref[...], marks_ref.shape)
    spread_weights(first_ref, spread_first)
    for head in range(heads):
        padded[head, 0 : 3 * margin] = jnp.zeros((3 * margin, band), F32)
        padded[head, 3 * margin :] = signal_ref[:, head * band : (head + 1) * band].astype(F32)
    pl.semaphore_wait(barrier, freq_count + tm_count - 2)

    def halo_copy():
        return pltpu.make_async_remote_copy(
            src_ref=signal_ref.at[pl.ds(count - 2 * margin, 2 * margin)],
            dst_ref=halo,
            send_sem=halo_sem.at[0],
            recv_sem=halo_sem.at[1],
            device_id={"tm": lax.rem(at_tm + 1, tm_count)},
            device_id_type=MESH,
        )

    @pl.when(at_tm < tm_count - 1)
    def _():
        halo_copy().start()

    def marks_copy(source, target):
        return pltpu.make_async_remote_copy(
            src_ref=marks_ref,
            dst_ref=marks.at[source],
            send_sem=b_send.at[target],
            recv_sem=b_recv.at[source],
            device_id={"tm": target},
            device_id_type=MESH,
        )

    for step in range(1, tm_count):
        marks_copy(at_tm, lax.rem(at_tm + step, tm_count)).start()
    marks[at_tm] = marks_ref[...]

    @pl.when(at_tm > 0)
    def _():
        halo_copy().wait_recv()
        for head in range(heads):
            padded[head, margin : 3 * margin] = halo[:, head * band : (head + 1) * band].astype(F32)

    columns = arrived.shape[2]
    size = first_ref.shape[2]
    sub = columns // groups
    parts = groups // sub
    part_heads = heads // parts
    deep = part_heads * band
    total_lanes = freq_count * columns
    channel = shuffle_ref.shape[1]
    spread = jnp.where(
        lax.broadcasted_iota(jnp.int32, (channel, total_lanes), 1) // sub
        == lax.broadcasted_iota(jnp.int32, (channel, total_lanes), 0),
        1.0,
        0.0,
    ).astype(BF16)
    taken = jnp.broadcast_to(shuffle_ref[...].astype(F32), (16, channel)).astype(BF16)
    lane = lax.broadcasted_iota(jnp.int32, (16, total_lanes), 1)
    taken = ordered_dot(taken, spread) + (lane % sub * size).astype(F32)
    for target in range(freq_count):
        source_ref[target] = taken[0:8, target * columns : (target + 1) * columns]

    def convolve_first(head, carry):
        total = jnp.zeros((rows, band), F32)
        for tap in range(taps):
            window = padded[head, margin - tap : margin - tap + rows].astype(BF16)
            total = total + ordered_dot(window, spread_first[head, tap])
        first[head] = (total / (1.0 + jnp.exp(-total))).astype(BF16)
        return carry

    row_ids = lax.broadcasted_iota(jnp.int32, (deep, columns), 0).astype(F32)

    def z_copy(source, target, piece):
        return pltpu.make_async_remote_copy(
            src_ref=sending.at[target * parts + piece],
            dst_ref=arrived.at[source * parts + piece],
            send_sem=z_send.at[target * parts + piece],
            recv_sem=z_recv.at[source * parts + piece],
            device_id={"freq": target},
            device_id_type=MESH,
        )

    def shuffle_for(target, piece):
        picks = jnp.where(row_ids == source_ref[target][0:1, :], 1.0, 0.0).astype(BF16)
        total = None
        for i in range(part_heads):
            term = ordered_dot(first[piece * part_heads + i], picks[i * band : (i + 1) * band])
            total = term if total is None else total + term
        return total.astype(BF16)

    def partner(step):
        chips = freq_count // 2
        chip = lax.rem(at_freq // 2 + step // 2 + 1, chips)
        return chip * 2 + lax.rem(at_freq % 2 + 1 + step % 2, 2)

    for piece in range(parts):
        lax.fori_loop(piece * part_heads, (piece + 1) * part_heads, convolve_first, 0)

        def shuffle_step(step, carry):
            target = partner(step)
            sending[target * parts + piece] = shuffle_for(target, piece)
            z_copy(at_freq, target, piece).start()
            return carry

        lax.fori_loop(0, freq_count - 1, shuffle_step, 0)
    for piece in range(parts):
        arrived[at_freq * parts + piece] = shuffle_for(at_freq, piece)
    for load in loads:
        load.wait()
    spread_weights(second_ref, spread_second)
    for step in range(freq_count - 1):
        for piece in range(parts):
            z_copy(partner(step), at_freq, piece).wait_recv()

    per_band = groups // heads
    chunk = per_band * sub
    lane_from = lax.broadcasted_iota(jnp.int32, (band, band), 0)
    lane_to = lax.broadcasted_iota(jnp.int32, (band, band), 1)
    wanted = (lane_from % chunk) // sub * size + lane_from // chunk * sub + lane_from % sub
    regroup = jnp.where(wanted == lane_to, 1.0, 0.0).astype(BF16)
    for head in range(heads):
        pieces = [
            arrived[source, :, head * chunk : (head + 1) * chunk]
            for source in range(freq_count * parts)
        ]
        shuffled[head] = ordered_dot(jnp.concatenate(pieces, axis=1), regroup)

    own_head, own_split = at_tm // splits, at_tm % splits

    def pair_copy(source, head):
        return pltpu.make_async_remote_copy(
            src_ref=pair_out.at[head],
            dst_ref=pairs.at[source],
            send_sem=kv_send.at[head],
            recv_sem=kv_recv.at[source],
            device_id={"tm": head * splits + own_split},
            device_id_type=MESH,
        )

    def forward_copy(source, step):
        return pltpu.make_async_remote_copy(
            src_ref=pairs.at[source],
            dst_ref=pairs.at[source],
            send_sem=forward_send.at[source * splits + step],
            recv_sem=kv_recv.at[source],
            device_id={"tm": own_head * splits + lax.rem(own_split + step, splits)},
            device_id_type=MESH,
        )

    def forward(source):
        for step in range(1, splits):
            forward_copy(source, step).start()

    def query_copy(source, head, split):
        target = head * splits + split
        return pltpu.make_async_remote_copy(
            src_ref=query_out.at[target],
            dst_ref=queries.at[source],
            send_sem=q_send.at[target],
            recv_sem=q_recv.at[source],
            device_id={"tm": target},
            device_id_type=MESH,
        )

    def project(head):
        total = padded[head, 3 * margin :]
        conv = jnp.zeros((count, band), F32)
        for tap in range(taps):
            window = shuffled[head, 2 * margin - tap : 2 * margin - tap + count].astype(BF16)
            conv = conv + ordered_dot(window, spread_second[head, tap])
        rounded = (total + conv).astype(BF16)
        resid[head] = rounded
        pair_out[head, :, 0:head_size] = ordered_dot(rounded, wk_ref[head]).astype(BF16)
        pair_out[head, :, head_size:] = ordered_dot(rounded, wv_ref[head]).astype(BF16)
        projected = ordered_dot(rounded, wq_ref[head]).astype(BF16)
        for split in range(splits):
            query_out[head * splits + split] = projected[split * part : (split + 1) * part]

    def project_step(step, carry):
        head = lax.rem(own_head + step, heads)
        project(head)
        pair_copy(at_tm, head).start()
        for split in range(splits):
            query_copy(at_tm, head, split).start()
        return carry

    lax.fori_loop(1, heads, project_step, 0)
    project(own_head)
    pairs[at_tm] = pair_out[own_head]
    queries[at_tm] = query_out[at_tm]
    forward(at_tm)
    for split in range(splits):

        @pl.when(own_split != split)
        def _():
            query_copy(at_tm, own_head, split).start()

    def att_copy(source, target):
        return pltpu.make_async_remote_copy(
            src_ref=att_out.at[target],
            dst_ref=att_in.at[source],
            send_sem=a_send.at[target],
            recv_sem=a_recv.at[source],
            device_id={"tm": target},
            device_id_type=MESH,
        )

    def pass_on(source):
        @pl.when(jnp.logical_and(own_split == source % splits, at_tm != source))
        def _():
            pair_copy(source, own_head).wait_recv()
            forward(source)

    def await_source(source):
        @pl.when(at_tm != source)
        def _():
            marks_copy(source, at_tm).wait_recv()
            query_copy(source, own_head, own_split).wait_recv()

        @pl.when(own_split != source % splits)
        def _():
            pair_copy(source, own_head).wait_recv()

    factor = math.log2(math.e) / math.sqrt(head_size)
    ahead = -(-BLOCK_MOST // LANES) * LANES
    contract = (((1,), (1,)), ((), ()))
    for source in range(min(splits, tm_count)):
        pass_on(source)
    await_source(0)
    for block in range(tm_count):
        if block + splits < tm_count:
            pass_on(block + splits)
        if block + 1 < tm_count:
            await_source(block + 1)
        asked = queries[block]
        near = pairs[block]
        near_marks = marks[block][0:1].astype(F32)
        if block + 1 < tm_count:
            near = jnp.concatenate([near, pairs[block + 1, 0:ahead]], axis=0)
            near_marks = jnp.concatenate(
                [near_marks, marks[block + 1][0:1, 0:ahead].astype(F32)], axis=1
            )
        offset = pl.multiple_of(own_split * part, LANES)
        mine = marks[block, 0:1, pl.ds(offset, part)].astype(F32)
        mine = jnp.transpose(jnp.broadcast_to(mine, (part, part)))[:, 0:1]
        near_scores = lax.dot_general(
            asked, near[:, 0:head_size], contract, preferred_element_type=F32
        )
        near_scores = jnp.where(near_marks <= mine, near_scores, -1e30)
        peak = jnp.max(near_scores, axis=1, keepdims=True)
        if block > 0:
            far = pairs[0:block].reshape(block * count, 2 * head_size)
            far_scores = lax.dot_general(
                asked, far[:, 0:head_size], contract, preferred_element_type=F32
            )
            peak = jnp.maximum(peak, jnp.max(far_scores, axis=1, keepdims=True))
        weights = jnp.exp2((near_scores - peak) * factor)
        total = jnp.sum(weights, axis=1, keepdims=True)
        summed = ordered_dot(weights.astype(BF16), near[:, head_size:])
        if block > 0:
            weights = jnp.exp2((far_scores - peak) * factor)
            total = total + jnp.sum(weights, axis=1, keepdims=True)
            summed = summed + ordered_dot(weights.astype(BF16), far[:, head_size:])
        att_out[block] = (summed / total).astype(BF16)

        @pl.when(at_tm != block)
        def _():
            att_copy(at_tm, block).start()

    att_in[at_tm] = att_out[at_tm]
    for source in range(tm_count):

        @pl.when(at_tm != source)
        def _():
            att_copy(source, at_tm).wait_recv()

        head, split = source // splits, source % splits
        top = split * part
        added = ordered_dot(att_in[source], wo_ref[head])
        out_ref[top : top + part, head * band : (head + 1) * band] = (
            resid[head, top : top + part].astype(F32) + added
        ).astype(BF16)

    @pl.when(at_tm < tm_count - 1)
    def _():
        halo_copy().wait_send()

    for step in range(freq_count - 1):
        for piece in range(parts):
            z_copy(at_freq, partner(step), piece).wait_send()
    for step in range(1, heads):
        pair_copy(at_tm, lax.rem(own_head + step, heads)).wait_send()
    for head in range(heads):
        for step in range(1, splits):
            forward_copy(head * splits + own_split, step).wait_send()
    for step in range(1, tm_count):
        target = lax.rem(at_tm + step, tm_count)
        marks_copy(at_tm, target).wait_send()
        query_copy(at_tm, target // splits, target % splits).wait_send()
        att_copy(at_tm, target).wait_send()


def per_device_fused(
    signal,
    conv_first,
    conv_second,
    shuffle,
    blocks,
    query_weight,
    key_weight,
    value_weight,
    out_weight,
):
    freq_count, tm_count = lax.axis_size("freq"), lax.axis_size("tm")
    count, width = signal.shape
    groups, taps, size, _ = conv_first.shape
    heads, band, head_size = query_weight.shape
    margin = taps - 1
    rows = count + 2 * margin
    part = count * heads // tm_count
    columns = LANES
    parts = groups * groups // columns
    vmem = pl.BlockSpec(memory_space=pltpu.VMEM)
    hbm = pl.BlockSpec(memory_space=pl.ANY)
    dma = pltpu.SemaphoreType.DMA
    return pl.pallas_call(
        functools.partial(layer_kernel, freq_count, tm_count),
        out_shape=jax.ShapeDtypeStruct((count, width), BF16),
        in_specs=[vmem] * 4 + [hbm] * 5,
        out_specs=vmem,
        scratch_shapes=[
            pltpu.VMEM(conv_second.shape, BF16),
            pltpu.VMEM(query_weight.shape, BF16),
            pltpu.VMEM(key_weight.shape, BF16),
            pltpu.VMEM(value_weight.shape, BF16),
            pltpu.VMEM(out_weight.shape, BF16),
            pltpu.VMEM((freq_count, 8, columns), F32),
            pltpu.VMEM((8, count), jnp.int32),
            pltpu.VMEM((heads, rows + margin, band), F32),
            pltpu.VMEM((heads, taps, band, band), BF16),
            pltpu.VMEM((heads, taps, band, band), BF16),
            pltpu.VMEM((2 * margin, width), BF16),
            pltpu.VMEM((heads, rows, band), BF16),
            pltpu.VMEM((freq_count * parts, rows, columns), BF16),
            pltpu.VMEM((freq_count * parts, rows, columns), BF16),
            pltpu.VMEM((heads, rows, band), F32),
            pltpu.VMEM((heads, count, band), BF16),
            pltpu.VMEM((heads, count, 2 * head_size), BF16),
            pltpu.VMEM((tm_count, part, head_size), BF16),
            pltpu.VMEM((tm_count, count, 2 * head_size), BF16),
            pltpu.VMEM((tm_count, part, head_size), BF16),
            pltpu.VMEM((tm_count, 8, count), jnp.int32),
            pltpu.VMEM((tm_count, part, head_size), BF16),
            pltpu.VMEM((tm_count, part, head_size), BF16),
            dma((2,)),
            dma((freq_count * parts,)),
            dma((freq_count * parts,)),
        ]
        + [dma((tm_count,))] * 8
        + [dma((tm_count * tm_count // heads,)), dma((5,))],
        compiler_params=pltpu.CompilerParams(
            collective_id=0, has_side_effects=True, vmem_limit_bytes=56 * 1024 * 1024
        ),
        cost_estimate=pl.CostEstimate(
            flops=10**10, bytes_accessed=8 * 10**6, transcendentals=2 * 10**6
        ),
    )(
        signal,
        conv_first,
        shuffle[None, :],
        blocks[None, :],
        conv_second,
        query_weight,
        key_weight,
        value_weight,
        out_weight,
    )


def fits_fused(signal, conv_first, query_weight):
    tm_count = lax.axis_size("tm")
    count = signal.shape[0]
    groups, taps, size, _ = conv_first.shape
    heads, band, head_size = query_weight.shape
    return (
        tm_count % heads == 0
        and (count * heads) % (LANES * tm_count) == 0
        and (groups * groups) % LANES == 0
        and LANES % groups == 0
        and heads % (groups * groups // LANES) == 0
        and lax.axis_size("freq") % 2 == 0
        and groups % heads == 0
        and heads * band == signal.shape[1]
        and (taps - 1) % 8 == 0
        and LANES % size == 0
        and band % LANES == 0
        and head_size % LANES == 0
        and size % 16 == 0
    )


def passed_along(block, axis, distance):
    devices = range(lax.axis_size(axis))
    route = [(i - distance, i) for i in devices if i - distance in devices]
    return lax.ppermute(block, axis, route)


def conv_local(padded, weights, length, form):
    margin = weights.shape[1] - 1
    result = None
    for offset in range(weights.shape[1]):
        term = jnp.einsum(
            form,
            padded[margin - offset : margin - offset + length],
            weights[:, offset],
            preferred_element_type=jnp.float32,
        )
        result = term if result is None else result + term
    return result


def split_range(count, width):
    return [(offset, min(offset + width, count)) for offset in range(0, count, width)]


def update_tile(state, query_part, query_marks, key_part, value_part, key_marks):
    peak, total, summed = state
    scale = 1.0 / math.sqrt(query_part.shape[2])
    scores = (
        jnp.einsum("qhd,khd->hqk", query_part, key_part, preferred_element_type=jnp.float32) * scale
    )
    seen = key_marks[None, None, :] <= query_marks[None, :, None]
    masked = jnp.where(seen, scores, jnp.float32(-1e30))
    new_peak = jnp.maximum(peak, jnp.max(masked, axis=2))
    weights = jnp.where(seen, jnp.exp(masked - new_peak[:, :, None]), jnp.float32(0.0))
    factor = jnp.exp(peak - new_peak)
    total = total * factor + jnp.sum(weights, axis=2)
    summed = summed * factor[:, :, None] + jnp.einsum(
        "hqk,khd->hqd", weights.astype(jnp.bfloat16), value_part, preferred_element_type=jnp.float32
    )
    return (new_peak, total, summed)


def unchanged(state, *others):
    return state


def make_fold(queries, query_marks):
    count = queries.shape[0]
    query_cuts = split_range(count, max(1, count // 2))

    def fold(carry, piece, start):
        key_rows, value_rows, key_marks = piece
        key_cuts = split_range(key_rows.shape[0], max(1, count // 2))
        peak, total, summed = carry
        results = []
        for top_row, end_row in query_cuts:
            state = (
                peak[:, top_row:end_row],
                total[:, top_row:end_row],
                summed[:, top_row:end_row],
            )
            for key_top, key_end in key_cuts:
                needed = jnp.min(key_marks[key_top:key_end]) <= jnp.max(
                    query_marks[top_row:end_row]
                )
                state = lax.cond(
                    needed,
                    update_tile,
                    unchanged,
                    state,
                    queries[top_row:end_row],
                    query_marks[top_row:end_row],
                    key_rows[key_top:key_end],
                    value_rows[key_top:key_end],
                    key_marks[key_top:key_end],
                )
            results.append(state)
        return tuple(
            (jnp.concatenate([entry[member] for entry in results], axis=1) for member in range(3))
        )

    return fold


def start_state(heads_here, count, head_size):
    return (
        jnp.full((heads_here, count), -1e30, jnp.float32),
        jnp.zeros((heads_here, count), jnp.float32),
        jnp.zeros((heads_here, count, head_size), jnp.float32),
    )


def finish(state):
    peak, total, summed = state
    return jnp.transpose(summed / total[:, :, None], (1, 0, 2)).astype(jnp.bfloat16)


def per_device_plain(
    signal,
    conv_first,
    conv_second,
    shuffle,
    blocks,
    query_weight,
    key_weight,
    value_weight,
    out_weight,
):
    count, width = signal.shape
    groups_here = conv_first.shape[0]
    group_size = conv_first.shape[2]
    margin = conv_first.shape[1] - 1
    local = signal.reshape(count, groups_here, group_size)
    selector = (shuffle[None, :] == jnp.arange(group_size, dtype=jnp.int32)[:, None]).astype(
        jnp.bfloat16
    )
    before = passed_along(local[count - 2 * margin :], "tm", 1)
    padded = jnp.concatenate([before, local], axis=0)
    first = jax.nn.silu(conv_local(padded, conv_first, count + margin, "tgi,gio->tgo")).astype(
        jnp.bfloat16
    )
    permuted = jnp.einsum(
        "tgj,jk->tgk", first, selector, preferred_element_type=jnp.float32
    ).astype(jnp.bfloat16)
    shuffled = lax.all_to_all(permuted, "freq", split_axis=2, concat_axis=1, tiled=True)
    second = conv_local(shuffled, conv_second, count, "tgk,kgo->tko")
    resid = (signal.astype(jnp.float32) + second.reshape(count, width)).astype(jnp.bfloat16)
    heads_here, band, head_size = query_weight.shape
    bands = resid.reshape(count, heads_here, band)
    queries = jnp.einsum(
        "thc,hcd->thd", bands, query_weight, preferred_element_type=jnp.float32
    ).astype(jnp.bfloat16)
    keys = jnp.einsum("thc,hcd->thd", bands, key_weight, preferred_element_type=jnp.float32).astype(
        jnp.bfloat16
    )
    values = jnp.einsum(
        "thc,hcd->thd", bands, value_weight, preferred_element_type=jnp.float32
    ).astype(jnp.bfloat16)
    initial = start_state(heads_here, count, head_size)
    fold = make_fold(queries, blocks)
    state = fold(
        initial,
        (
            lax.all_gather(keys, "tm", axis=0, tiled=True),
            lax.all_gather(values, "tm", axis=0, tiled=True),
            lax.all_gather(blocks, "tm", axis=0, tiled=True),
        ),
        jnp.int32(0),
    )
    attended = finish(state)
    added = jnp.einsum("thd,hdc->thc", attended, out_weight, preferred_element_type=jnp.float32)
    return (resid.astype(jnp.float32) + added.reshape(count, width)).astype(jnp.bfloat16)


def per_device(*args):
    if fits_fused(args[0], args[1], args[5]):
        return per_device_fused(*args)
    return per_device_plain(*args)


def solution(mesh):
    in_specs = (
        P("tm", "freq"),
        P("freq", None, None, None),
        P("freq", None, None, None),
        P(),
        P("tm"),
        P("freq", None, None),
        P("freq", None, None),
        P("freq", None, None),
        P("freq", None, None),
    )
    out_specs = P("tm", "freq")
    return jax.shard_map(
        per_device, mesh=mesh, in_specs=in_specs, out_specs=out_specs, check_vma=False
    )
```

```python
import functools
import math

import jax
import jax.numpy as jnp
from jax import lax
from jax.experimental import pallas as pl
from jax.experimental.pallas import tpu as pltpu
from jax.sharding import PartitionSpec as P

MESH = pl.DeviceIdType.MESH
BLOCK_MOST = 64
LANES = 128
F32 = jnp.float32
BF16 = jnp.bfloat16


def ordered_dot(a, b):
    return jnp.dot(a, b, preferred_element_type=F32)


def spread_weights(weights_ref, spread_ref):
    spread_ref[...] = jnp.zeros_like(spread_ref)
    groups, taps, size, _ = weights_ref.shape
    per_band = spread_ref.shape[2] // size
    per_tile = LANES // size
    for group in range(groups):
        place = group % per_band
        tile, slot = place // per_tile, place % per_tile
        block = weights_ref[group]
        parts = [block if i == slot else jnp.zeros_like(block) for i in range(per_tile)]
        spread_ref[
            group // per_band,
            :,
            place * size : (place + 1) * size,
            tile * LANES : (tile + 1) * LANES,
        ] = jnp.concatenate(parts, axis=2)


def layer_kernel(
    freq_count,
    tm_count,
    signal_ref,
    shuffle_ref,
    blocks_ref,
    first_hbm,
    second_hbm,
    wq_hbm,
    wk_hbm,
    wv_hbm,
    wo_hbm,
    out_ref,
    first_ref,
    second_ref,
    wq_ref,
    wk_ref,
    wv_ref,
    wo_ref,
    picks,
    marks_ref,
    padded,
    spread_first,
    spread_second,
    halo,
    first,
    sending,
    arrived,
    shuffled,
    resid,
    pair_out,
    query_out,
    pairs,
    queries,
    marks,
    att_out,
    att_in,
    halo_sem,
    z_send,
    z_recv,
    b_send,
    b_recv,
    kv_send,
    kv_recv,
    q_send,
    q_recv,
    a_send,
    a_recv,
    forward_send,
    load_sem,
):
    at_freq, at_tm = lax.axis_index("freq"), lax.axis_index("tm")
    count = signal_ref.shape[0]
    heads, band, head_size = wq_ref.shape
    taps = first_ref.shape[1]
    groups = first_ref.shape[0]
    margin = taps - 1
    rows = count + 2 * margin
    splits = tm_count // heads
    part = count // splits

    barrier = pltpu.get_barrier_semaphore()
    for step in range(1, freq_count):
        pl.semaphore_signal(
            barrier,
            inc=1,
            device_id={"freq": lax.rem(at_freq + step, freq_count)},
            device_id_type=MESH,
        )
    for step in range(1, tm_count):
        pl.semaphore_signal(
            barrier,
            inc=1,
            device_id={"tm": lax.rem(at_tm + step, tm_count)},
            device_id_type=MESH,
        )
    loads = [
        pltpu.make_async_copy(whole, local, load_sem.at[i])
        for i, (whole, local) in enumerate(
            (
                (first_hbm, first_ref),
                (second_hbm, second_ref),
                (wq_hbm, wq_ref),
                (wk_hbm, wk_ref),
                (wv_hbm, wv_ref),
                (wo_hbm, wo_ref),
            )
        )
    ]
    for load in loads:
        load.start()
    marks_ref[...] = jnp.broadcast_to(blocks_ref[...], marks_ref.shape)
    for head in range(heads):
        padded[head, 0 : 3 * margin] = jnp.zeros((3 * margin, band), F32)
        padded[head, 3 * margin :] = signal_ref[:, head * band : (head + 1) * band].astype(F32)

    columns = picks.shape[2]
    size = first_ref.shape[2]
    sub = columns // groups
    parts = groups // sub
    part_heads = heads // parts
    deep = part_heads * band
    total_lanes = freq_count * columns
    channel = shuffle_ref.shape[1]
    spread = jnp.where(
        lax.broadcasted_iota(jnp.int32, (channel, total_lanes), 1) // sub
        == lax.broadcasted_iota(jnp.int32, (channel, total_lanes), 0),
        1.0,
        0.0,
    ).astype(BF16)
    taken = jnp.broadcast_to(shuffle_ref[...].astype(F32), (16, channel)).astype(BF16)
    lane = lax.broadcasted_iota(jnp.int32, (16, total_lanes), 1)
    taken = ordered_dot(taken, spread) + (lane % sub * size).astype(F32)
    row_ids = lax.broadcasted_iota(jnp.int32, (deep, columns), 0).astype(F32)
    for target in range(freq_count):
        source = taken[0:1, target * columns : (target + 1) * columns]
        picks[target] = jnp.where(row_ids == source, 1.0, 0.0).astype(BF16)
    pl.semaphore_wait(barrier, freq_count + tm_count - 2)

    def halo_copy():
        return pltpu.make_async_remote_copy(
            src_ref=signal_ref.at[pl.ds(count - 2 * margin, 2 * margin)],
            dst_ref=halo,
            send_sem=halo_sem.at[0],
            recv_sem=halo_sem.at[1],
            device_id={"tm": lax.rem(at_tm + 1, tm_count)},
            device_id_type=MESH,
        )

    @pl.when(at_tm < tm_count - 1)
    def _():
        halo_copy().start()

    def marks_copy(source, target):
        return pltpu.make_async_remote_copy(
            src_ref=marks_ref,
            dst_ref=marks.at[source],
            send_sem=b_send.at[target],
            recv_sem=b_recv.at[source],
            device_id={"tm": target},
            device_id_type=MESH,
        )

    for step in range(1, tm_count):
        marks_copy(at_tm, lax.rem(at_tm + step, tm_count)).start()
    marks[at_tm] = marks_ref[...]
    loads[0].wait()
    spread_weights(first_ref, spread_first)

    @pl.when(at_tm > 0)
    def _():
        halo_copy().wait_recv()
        for head in range(heads):
            padded[head, margin : 3 * margin] = halo[:, head * band : (head + 1) * band].astype(F32)

    def convolve(source, head, top, length, spread_ref):
        windows = [source[head, top - tap : top - tap + length] for tap in range(taps)]
        windows = jnp.concatenate([window.astype(BF16) for window in windows], axis=1)
        return ordered_dot(windows, spread_ref[head].reshape(taps * band, band))

    cuts = [(0, 2 * margin + part)] + [
        (2 * margin + i * part, part) for i in range(1, splits)
    ]

    def z_copy(source, target, half):
        top, length = cuts[half]
        return pltpu.make_async_remote_copy(
            src_ref=sending.at[target, pl.ds(top, length)],
            dst_ref=arrived.at[source, pl.ds(top, length)],
            send_sem=z_send.at[target * splits + half],
            recv_sem=z_recv.at[source * splits + half],
            device_id={"freq": target},
            device_id_type=MESH,
        )

    def shuffle_for(target, half, out):
        top, length = cuts[half]
        for piece in range(parts):
            held = [
                first[piece * part_heads + i, top : top + length] for i in range(part_heads)
            ]
            out[target, top : top + length, piece * columns : (piece + 1) * columns] = ordered_dot(
                jnp.concatenate(held, axis=1), picks[target]
            ).astype(BF16)

    def partner(step):
        chips = freq_count // 2
        chip = lax.rem(at_freq // 2 + step // 2 + 1, chips)
        return chip * 2 + lax.rem(at_freq % 2 + 1 + step % 2, 2)

    for half in range(splits):
        top, length = cuts[half]

        def convolve_first(head, carry):
            total = convolve(padded, head, margin + top, length, spread_first)
            first[head, top : top + length] = (total / (1.0 + jnp.exp(-total))).astype(BF16)
            return carry

        lax.fori_loop(0, heads, convolve_first, 0)

        def shuffle_step(step, carry):
            target = partner(step)
            shuffle_for(target, half, sending)
            z_copy(at_freq, target, half).start()
            return carry

        lax.fori_loop(0, freq_count - 1, shuffle_step, 0)
    for half in range(splits):
        shuffle_for(at_freq, half, arrived)
    for load in loads[1:]:
        load.wait()
    spread_weights(second_ref, spread_second)

    per_band = groups // heads
    chunk = per_band * sub
    lane_from = lax.broadcasted_iota(jnp.int32, (band, band), 0)
    lane_to = lax.broadcasted_iota(jnp.int32, (band, band), 1)
    wanted = (lane_from % chunk) // sub * size + lane_from // chunk * sub + lane_from % sub
    regroup = jnp.where(wanted == lane_to, 1.0, 0.0).astype(BF16)

    def regroup_half(half):
        top, length = cuts[half]
        for step in range(freq_count - 1):
            z_copy(partner(step), at_freq, half).wait_recv()
        for head in range(heads):
            pieces = [
                arrived[
                    source,
                    top : top + length,
                    piece * columns + head * chunk : piece * columns + (head + 1) * chunk,
                ]
                for source in range(freq_count)
                for piece in range(parts)
            ]
            shuffled[head, top : top + length] = ordered_dot(
                jnp.concatenate(pieces, axis=1), regroup
            )

    own_head, own_split = at_tm // splits, at_tm % splits

    def pair_copy(source, head, half):
        return pltpu.make_async_remote_copy(
            src_ref=pair_out.at[head, pl.ds(half * part, part)],
            dst_ref=pairs.at[source, pl.ds(half * part, part)],
            send_sem=kv_send.at[head * splits + half],
            recv_sem=kv_recv.at[source * splits + half],
            device_id={"tm": head * splits + own_split},
            device_id_type=MESH,
        )

    def forward_copy(source, step, half):
        return pltpu.make_async_remote_copy(
            src_ref=pairs.at[source, pl.ds(half * part, part)],
            dst_ref=pairs.at[source, pl.ds(half * part, part)],
            send_sem=forward_send.at[(source * splits + step) * splits + half],
            recv_sem=kv_recv.at[source * splits + half],
            device_id={"tm": own_head * splits + lax.rem(own_split + step, splits)},
            device_id_type=MESH,
        )

    def forward(source, half):
        for step in range(1, splits):
            forward_copy(source, step, half).start()

    def query_copy(source, head, split):
        target = head * splits + split
        return pltpu.make_async_remote_copy(
            src_ref=query_out.at[target],
            dst_ref=queries.at[source],
            send_sem=q_send.at[target],
            recv_sem=q_recv.at[source],
            device_id={"tm": target},
            device_id_type=MESH,
        )

    def project(head, half):
        top = half * part
        total = padded[head, 3 * margin + top : 3 * margin + top + part]
        total = total + convolve(shuffled, head, 2 * margin + top, part, spread_second)
        rounded = total.astype(BF16)
        resid[head, top : top + part] = rounded
        pair_out[head, top : top + part, 0:head_size] = ordered_dot(
            rounded, wk_ref[head]
        ).astype(BF16)
        pair_out[head, top : top + part, head_size:] = ordered_dot(
            rounded, wv_ref[head]
        ).astype(BF16)
        query_out[head * splits + half] = ordered_dot(rounded, wq_ref[head]).astype(BF16)

    for half in range(splits):
        regroup_half(half)

        def project_step(step, carry):
            head = lax.rem(own_head + step, heads)
            project(head, half)
            pair_copy(at_tm, head, half).start()
            query_copy(at_tm, head, half).start()
            return carry

        lax.fori_loop(1, heads, project_step, 0)
        project(own_head, half)
        top = half * part
        pairs[at_tm, top : top + part] = pair_out[own_head, top : top + part]
        forward(at_tm, half)

        @pl.when(own_split != half)
        def _():
            query_copy(at_tm, own_head, half).start()

    queries[at_tm] = query_out[at_tm]

    def att_copy(source, target):
        return pltpu.make_async_remote_copy(
            src_ref=att_out.at[target],
            dst_ref=att_in.at[source],
            send_sem=a_send.at[target],
            recv_sem=a_recv.at[source],
            device_id={"tm": target},
            device_id_type=MESH,
        )

    def pass_on(source):
        @pl.when(jnp.logical_and(own_split == source % splits, at_tm != source))
        def _():
            for half in range(splits):
                pair_copy(source, own_head, half).wait_recv()
                forward(source, half)

    def await_source(source):
        @pl.when(at_tm != source)
        def _():
            marks_copy(source, at_tm).wait_recv()
            query_copy(source, own_head, own_split).wait_recv()

        @pl.when(own_split != source % splits)
        def _():
            for half in range(splits):
                pair_copy(source, own_head, half).wait_recv()

    factor = math.log2(math.e) / math.sqrt(head_size)
    ahead = -(-BLOCK_MOST // LANES) * LANES
    contract = (((1,), (1,)), ((), ()))
    for source in range(min(splits, tm_count)):
        pass_on(source)
    await_source(0)
    for block in range(tm_count):
        if block + splits < tm_count:
            pass_on(block + splits)
        if block + 1 < tm_count:
            await_source(block + 1)
        asked = queries[block]
        near = pairs[block]
        near_marks = marks[block][0:1].astype(F32)
        if block + 1 < tm_count:
            near = jnp.concatenate([near, pairs[block + 1, 0:ahead]], axis=0)
            near_marks = jnp.concatenate(
                [near_marks, marks[block + 1][0:1, 0:ahead].astype(F32)], axis=1
            )
        offset = pl.multiple_of(own_split * part, LANES)
        mine = marks[block, 0:1, pl.ds(offset, part)].astype(F32)
        mine = jnp.transpose(jnp.broadcast_to(mine, (part, part)))[:, 0:1]
        near_scores = lax.dot_general(
            asked, near[:, 0:head_size], contract, preferred_element_type=F32
        )
        near_scores = jnp.where(near_marks <= mine, near_scores, -1e30)
        peak = jnp.max(near_scores, axis=1, keepdims=True)
        if block > 0:
            far = pairs[0:block].reshape(block * count, 2 * head_size)
            far_scores = lax.dot_general(
                asked, far[:, 0:head_size], contract, preferred_element_type=F32
            )
            peak = jnp.maximum(peak, jnp.max(far_scores, axis=1, keepdims=True))
        weights = jnp.exp2((near_scores - peak) * factor)
        total = jnp.sum(weights, axis=1, keepdims=True)
        summed = ordered_dot(weights.astype(BF16), near[:, head_size:])
        if block > 0:
            weights = jnp.exp2((far_scores - peak) * factor)
            total = total + jnp.sum(weights, axis=1, keepdims=True)
            summed = summed + ordered_dot(weights.astype(BF16), far[:, head_size:])
        att_out[block] = (summed / total).astype(BF16)

        @pl.when(at_tm != block)
        def _():
            att_copy(at_tm, block).start()

    att_in[at_tm] = att_out[at_tm]
    for source in range(tm_count):

        @pl.when(at_tm != source)
        def _():
            att_copy(source, at_tm).wait_recv()

        head, split = source // splits, source % splits
        top = split * part
        added = ordered_dot(att_in[source], wo_ref[head])
        out_ref[top : top + part, head * band : (head + 1) * band] = (
            resid[head, top : top + part].astype(F32) + added
        ).astype(BF16)

    @pl.when(at_tm < tm_count - 1)
    def _():
        halo_copy().wait_send()

    for half in range(splits):
        for step in range(freq_count - 1):
            z_copy(at_freq, partner(step), half).wait_send()
        for step in range(1, heads):
            pair_copy(at_tm, lax.rem(own_head + step, heads), half).wait_send()
        for head in range(heads):
            for step in range(1, splits):
                forward_copy(head * splits + own_split, step, half).wait_send()
    for step in range(1, tm_count):
        target = lax.rem(at_tm + step, tm_count)
        marks_copy(at_tm, target).wait_send()
        query_copy(at_tm, target // splits, target % splits).wait_send()
        att_copy(at_tm, target).wait_send()


def per_device_fused(
    signal,
    conv_first,
    conv_second,
    shuffle,
    blocks,
    query_weight,
    key_weight,
    value_weight,
    out_weight,
):
    freq_count, tm_count = lax.axis_size("freq"), lax.axis_size("tm")
    count, width = signal.shape
    groups, taps, size, _ = conv_first.shape
    heads, band, head_size = query_weight.shape
    margin = taps - 1
    rows = count + 2 * margin
    part = count * heads // tm_count
    splits = tm_count // heads
    columns = groups * groups
    deep = heads * band * LANES // columns
    vmem = pl.BlockSpec(memory_space=pltpu.VMEM)
    hbm = pl.BlockSpec(memory_space=pl.ANY)
    dma = pltpu.SemaphoreType.DMA
    return pl.pallas_call(
        functools.partial(layer_kernel, freq_count, tm_count),
        out_shape=jax.ShapeDtypeStruct((count, width), BF16),
        in_specs=[vmem] * 3 + [hbm] * 6,
        out_specs=vmem,
        scratch_shapes=[
            pltpu.VMEM(conv_first.shape, BF16),
            pltpu.VMEM(conv_second.shape, BF16),
            pltpu.VMEM(query_weight.shape, BF16),
            pltpu.VMEM(key_weight.shape, BF16),
            pltpu.VMEM(value_weight.shape, BF16),
            pltpu.VMEM(out_weight.shape, BF16),
            pltpu.VMEM((freq_count, deep, LANES), BF16),
            pltpu.VMEM((8, count), jnp.int32),
            pltpu.VMEM((heads, rows + margin, band), F32),
            pltpu.VMEM((heads, taps, band, band), BF16),
            pltpu.VMEM((heads, taps, band, band), BF16),
            pltpu.VMEM((2 * margin, width), BF16),
            pltpu.VMEM((heads, rows, band), BF16),
            pltpu.VMEM((freq_count, rows, columns), BF16),
            pltpu.VMEM((freq_count, rows, columns), BF16),
            pltpu.VMEM((heads, rows, band), F32),
            pltpu.VMEM((heads, count, band), BF16),
            pltpu.VMEM((heads, count, 2 * head_size), BF16),
            pltpu.VMEM((tm_count, part, head_size), BF16),
            pltpu.VMEM((tm_count, count, 2 * head_size), BF16),
            pltpu.VMEM((tm_count, part, head_size), BF16),
            pltpu.VMEM((tm_count, 8, count), jnp.int32),
            pltpu.VMEM((tm_count, part, head_size), BF16),
            pltpu.VMEM((tm_count, part, head_size), BF16),
            dma((2,)),
            dma((freq_count * splits,)),
            dma((freq_count * splits,)),
        ]
        + [dma((tm_count,))] * 2
        + [dma((tm_count,)), dma((tm_count * splits,))]
        + [dma((tm_count,))] * 4
        + [dma((tm_count * splits * splits,)), dma((6,))],
        compiler_params=pltpu.CompilerParams(
            collective_id=0, has_side_effects=True, vmem_limit_bytes=56 * 1024 * 1024
        ),
        cost_estimate=pl.CostEstimate(
            flops=10**10, bytes_accessed=8 * 10**6, transcendentals=2 * 10**6
        ),
    )(
        signal,
        shuffle[None, :],
        blocks[None, :],
        conv_first,
        conv_second,
        query_weight,
        key_weight,
        value_weight,
        out_weight,
    )


def fits_fused(signal, conv_first, query_weight):
    tm_count = lax.axis_size("tm")
    count = signal.shape[0]
    groups, taps, size, _ = conv_first.shape
    heads, band, head_size = query_weight.shape
    return (
        tm_count % heads == 0
        and (count * heads) % (LANES * tm_count) == 0
        and (groups * groups) % LANES == 0
        and LANES % groups == 0
        and heads % (groups * groups // LANES) == 0
        and lax.axis_size("freq") % 2 == 0
        and groups % heads == 0
        and heads * band == signal.shape[1]
        and (taps - 1) % 8 == 0
        and LANES % size == 0
        and band % LANES == 0
        and head_size % LANES == 0
        and size % 16 == 0
    )


def passed_along(block, axis, distance):
    devices = range(lax.axis_size(axis))
    route = [(i - distance, i) for i in devices if i - distance in devices]
    return lax.ppermute(block, axis, route)


def conv_local(padded, weights, length, form):
    margin = weights.shape[1] - 1
    result = None
    for offset in range(weights.shape[1]):
        term = jnp.einsum(
            form,
            padded[margin - offset : margin - offset + length],
            weights[:, offset],
            preferred_element_type=jnp.float32,
        )
        result = term if result is None else result + term
    return result


def split_range(count, width):
    return [(offset, min(offset + width, count)) for offset in range(0, count, width)]


def update_tile(state, query_part, query_marks, key_part, value_part, key_marks):
    peak, total, summed = state
    scale = 1.0 / math.sqrt(query_part.shape[2])
    scores = (
        jnp.einsum("qhd,khd->hqk", query_part, key_part, preferred_element_type=jnp.float32) * scale
    )
    seen = key_marks[None, None, :] <= query_marks[None, :, None]
    masked = jnp.where(seen, scores, jnp.float32(-1e30))
    new_peak = jnp.maximum(peak, jnp.max(masked, axis=2))
    weights = jnp.where(seen, jnp.exp(masked - new_peak[:, :, None]), jnp.float32(0.0))
    factor = jnp.exp(peak - new_peak)
    total = total * factor + jnp.sum(weights, axis=2)
    summed = summed * factor[:, :, None] + jnp.einsum(
        "hqk,khd->hqd", weights.astype(jnp.bfloat16), value_part, preferred_element_type=jnp.float32
    )
    return (new_peak, total, summed)


def unchanged(state, *others):
    return state


def make_fold(queries, query_marks):
    count = queries.shape[0]
    query_cuts = split_range(count, max(1, count // 2))

    def fold(carry, piece, start):
        key_rows, value_rows, key_marks = piece
        key_cuts = split_range(key_rows.shape[0], max(1, count // 2))
        peak, total, summed = carry
        results = []
        for top_row, end_row in query_cuts:
            state = (
                peak[:, top_row:end_row],
                total[:, top_row:end_row],
                summed[:, top_row:end_row],
            )
            for key_top, key_end in key_cuts:
                needed = jnp.min(key_marks[key_top:key_end]) <= jnp.max(
                    query_marks[top_row:end_row]
                )
                state = lax.cond(
                    needed,
                    update_tile,
                    unchanged,
                    state,
                    queries[top_row:end_row],
                    query_marks[top_row:end_row],
                    key_rows[key_top:key_end],
                    value_rows[key_top:key_end],
                    key_marks[key_top:key_end],
                )
            results.append(state)
        return tuple(
            (jnp.concatenate([entry[member] for entry in results], axis=1) for member in range(3))
        )

    return fold


def start_state(heads_here, count, head_size):
    return (
        jnp.full((heads_here, count), -1e30, jnp.float32),
        jnp.zeros((heads_here, count), jnp.float32),
        jnp.zeros((heads_here, count, head_size), jnp.float32),
    )


def finish(state):
    peak, total, summed = state
    return jnp.transpose(summed / total[:, :, None], (1, 0, 2)).astype(jnp.bfloat16)


def per_device_plain(
    signal,
    conv_first,
    conv_second,
    shuffle,
    blocks,
    query_weight,
    key_weight,
    value_weight,
    out_weight,
):
    count, width = signal.shape
    groups_here = conv_first.shape[0]
    group_size = conv_first.shape[2]
    margin = conv_first.shape[1] - 1
    local = signal.reshape(count, groups_here, group_size)
    selector = (shuffle[None, :] == jnp.arange(group_size, dtype=jnp.int32)[:, None]).astype(
        jnp.bfloat16
    )
    before = passed_along(local[count - 2 * margin :], "tm", 1)
    padded = jnp.concatenate([before, local], axis=0)
    first = jax.nn.silu(conv_local(padded, conv_first, count + margin, "tgi,gio->tgo")).astype(
        jnp.bfloat16
    )
    permuted = jnp.einsum(
        "tgj,jk->tgk", first, selector, preferred_element_type=jnp.float32
    ).astype(jnp.bfloat16)
    shuffled = lax.all_to_all(permuted, "freq", split_axis=2, concat_axis=1, tiled=True)
    second = conv_local(shuffled, conv_second, count, "tgk,kgo->tko")
    resid = (signal.astype(jnp.float32) + second.reshape(count, width)).astype(jnp.bfloat16)
    heads_here, band, head_size = query_weight.shape
    bands = resid.reshape(count, heads_here, band)
    queries = jnp.einsum(
        "thc,hcd->thd", bands, query_weight, preferred_element_type=jnp.float32
    ).astype(jnp.bfloat16)
    keys = jnp.einsum("thc,hcd->thd", bands, key_weight, preferred_element_type=jnp.float32).astype(
        jnp.bfloat16
    )
    values = jnp.einsum(
        "thc,hcd->thd", bands, value_weight, preferred_element_type=jnp.float32
    ).astype(jnp.bfloat16)
    initial = start_state(heads_here, count, head_size)
    fold = make_fold(queries, blocks)
    state = fold(
        initial,
        (
            lax.all_gather(keys, "tm", axis=0, tiled=True),
            lax.all_gather(values, "tm", axis=0, tiled=True),
            lax.all_gather(blocks, "tm", axis=0, tiled=True),
        ),
        jnp.int32(0),
    )
    attended = finish(state)
    added = jnp.einsum("thd,hdc->thc", attended, out_weight, preferred_element_type=jnp.float32)
    return (resid.astype(jnp.float32) + added.reshape(count, width)).astype(jnp.bfloat16)


def per_device(*args):
    if fits_fused(args[0], args[1], args[5]):
        return per_device_fused(*args)
    return per_device_plain(*args)


def solution(mesh):
    in_specs = (
        P("tm", "freq"),
        P("freq", None, None, None),
        P("freq", None, None, None),
        P(),
        P("tm"),
        P("freq", None, None),
        P("freq", None, None),
        P("freq", None, None),
        P("freq", None, None),
    )
    out_specs = P("tm", "freq")
    return jax.shard_map(
        per_device, mesh=mesh, in_specs=in_specs, out_specs=out_specs, check_vma=False
    )
```

```python
import functools
import math

import jax
import jax.numpy as jnp
from jax import lax
from jax.experimental import pallas as pl
from jax.experimental.pallas import tpu as pltpu
from jax.sharding import PartitionSpec as P

MESH = pl.DeviceIdType.MESH
BLOCK_MOST = 64
LANES = 128
F32 = jnp.float32
BF16 = jnp.bfloat16


def ordered_dot(a, b):
    return jnp.dot(a, b, preferred_element_type=F32)


def spread_weights(weights_ref, spread_ref):
    spread_ref[...] = jnp.zeros_like(spread_ref)
    groups, taps, size, _ = weights_ref.shape
    per_band = spread_ref.shape[2] // size
    per_tile = LANES // size
    for group in range(groups):
        place = group % per_band
        tile, slot = place // per_tile, place % per_tile
        block = weights_ref[group]
        parts = [block if i == slot else jnp.zeros_like(block) for i in range(per_tile)]
        spread_ref[
            group // per_band,
            :,
            place * size : (place + 1) * size,
            tile * LANES : (tile + 1) * LANES,
        ] = jnp.concatenate(parts, axis=2)


def layer_kernel(
    freq_count,
    tm_count,
    signal_ref,
    shuffle_ref,
    blocks_ref,
    first_hbm,
    second_hbm,
    wq_hbm,
    wk_hbm,
    wv_hbm,
    wo_hbm,
    out_ref,
    first_ref,
    second_ref,
    wq_ref,
    wk_ref,
    wv_ref,
    wo_ref,
    picks,
    marks_ref,
    padded,
    spread_first,
    spread_second,
    halo,
    first,
    sending,
    arrived,
    shuffled,
    resid,
    pair_out,
    query_out,
    pairs,
    queries,
    marks,
    att_out,
    att_in,
    halo_sem,
    z_send,
    z_recv,
    b_send,
    b_recv,
    kv_send,
    kv_recv,
    q_send,
    q_recv,
    a_send,
    a_recv,
    forward_send,
    load_sem,
):
    at_freq, at_tm = lax.axis_index("freq"), lax.axis_index("tm")
    count = signal_ref.shape[0]
    heads, band, head_size = wq_ref.shape
    taps = first_ref.shape[1]
    groups = first_ref.shape[0]
    margin = taps - 1
    rows = count + 2 * margin
    splits = tm_count // heads
    part = count // splits

    barrier = pltpu.get_barrier_semaphore()
    for step in range(1, freq_count):
        pl.semaphore_signal(
            barrier,
            inc=1,
            device_id={"freq": lax.rem(at_freq + step, freq_count)},
            device_id_type=MESH,
        )
    for step in range(1, tm_count):
        pl.semaphore_signal(
            barrier,
            inc=1,
            device_id={"tm": lax.rem(at_tm + step, tm_count)},
            device_id_type=MESH,
        )
    loads = [
        pltpu.make_async_copy(whole, local, load_sem.at[i])
        for i, (whole, local) in enumerate(
            (
                (first_hbm, first_ref),
                (second_hbm, second_ref),
                (wq_hbm, wq_ref),
                (wk_hbm, wk_ref),
                (wv_hbm, wv_ref),
                (wo_hbm, wo_ref),
            )
        )
    ]
    loads[0].start()
    marks_ref[...] = jnp.broadcast_to(blocks_ref[...], marks_ref.shape)
    for head in range(heads):
        padded[head, 0 : 3 * margin] = jnp.zeros((3 * margin, band), F32)
        padded[head, 3 * margin :] = signal_ref[:, head * band : (head + 1) * band].astype(F32)

    columns = picks.shape[2]
    size = first_ref.shape[2]
    sub = columns // groups
    parts = groups // sub
    part_heads = heads // parts
    deep = part_heads * band
    total_lanes = freq_count * columns
    channel = shuffle_ref.shape[1]
    spread = jnp.where(
        lax.broadcasted_iota(jnp.int32, (channel, total_lanes), 1) // sub
        == lax.broadcasted_iota(jnp.int32, (channel, total_lanes), 0),
        1.0,
        0.0,
    ).astype(BF16)
    taken = jnp.broadcast_to(shuffle_ref[...].astype(F32), (16, channel)).astype(BF16)
    lane = lax.broadcasted_iota(jnp.int32, (16, total_lanes), 1)
    taken = ordered_dot(taken, spread) + (lane % sub * size).astype(F32)
    row_ids = lax.broadcasted_iota(jnp.int32, (deep, columns), 0).astype(F32)
    for target in range(freq_count):
        source = taken[0:1, target * columns : (target + 1) * columns]
        picks[target] = jnp.where(row_ids == source, 1.0, 0.0).astype(BF16)
    pl.semaphore_wait(barrier, freq_count + tm_count - 2)

    def halo_copy():
        return pltpu.make_async_remote_copy(
            src_ref=signal_ref.at[pl.ds(count - 2 * margin, 2 * margin)],
            dst_ref=halo,
            send_sem=halo_sem.at[0],
            recv_sem=halo_sem.at[1],
            device_id={"tm": lax.rem(at_tm + 1, tm_count)},
            device_id_type=MESH,
        )

    @pl.when(at_tm < tm_count - 1)
    def _():
        halo_copy().start()

    def marks_copy(source, target):
        return pltpu.make_async_remote_copy(
            src_ref=marks_ref,
            dst_ref=marks.at[source],
            send_sem=b_send.at[target],
            recv_sem=b_recv.at[source],
            device_id={"tm": target},
            device_id_type=MESH,
        )

    for step in range(1, tm_count):
        marks_copy(at_tm, lax.rem(at_tm + step, tm_count)).start()
    marks[at_tm] = marks_ref[...]
    loads[0].wait()
    for load in loads[1:]:
        load.start()
    spread_weights(first_ref, spread_first)

    @pl.when(at_tm > 0)
    def _():
        halo_copy().wait_recv()
        for head in range(heads):
            padded[head, margin : 3 * margin] = halo[:, head * band : (head + 1) * band].astype(F32)

    def convolve(source, head, top, length, spread_ref):
        windows = [source[head, top - tap : top - tap + length] for tap in range(taps)]
        windows = jnp.concatenate([window.astype(BF16) for window in windows], axis=1)
        return ordered_dot(windows, spread_ref[head].reshape(taps * band, band))

    cuts = [(0, 2 * margin + part)] + [
        (2 * margin + i * part, part) for i in range(1, splits)
    ]

    def z_copy(source, target, half):
        top, length = cuts[half]
        return pltpu.make_async_remote_copy(
            src_ref=sending.at[target, pl.ds(top, length)],
            dst_ref=arrived.at[source, pl.ds(top, length)],
            send_sem=z_send.at[target * splits + half],
            recv_sem=z_recv.at[source * splits + half],
            device_id={"freq": target},
            device_id_type=MESH,
        )

    def shuffle_for(target, half, out):
        top, length = cuts[half]
        for piece in range(parts):
            held = [
                first[piece * part_heads + i, top : top + length] for i in range(part_heads)
            ]
            out[target, top : top + length, piece * columns : (piece + 1) * columns] = ordered_dot(
                jnp.concatenate(held, axis=1), picks[target]
            ).astype(BF16)

    def partner(step):
        chips = freq_count // 2
        chip = lax.rem(at_freq // 2 + step // 2 + 1, chips)
        return chip * 2 + lax.rem(at_freq % 2 + 1 + step % 2, 2)

    for half in range(splits):
        top, length = cuts[half]

        def convolve_first(head, carry):
            total = convolve(padded, head, margin + top, length, spread_first)
            first[head, top : top + length] = (total / (1.0 + jnp.exp(-total))).astype(BF16)
            return carry

        lax.fori_loop(0, heads, convolve_first, 0)

        def shuffle_step(step, carry):
            target = partner(step)
            shuffle_for(target, half, sending)
            z_copy(at_freq, target, half).start()
            return carry

        lax.fori_loop(0, freq_count - 1, shuffle_step, 0)
    for half in range(splits):
        shuffle_for(at_freq, half, arrived)
    for load in loads[1:]:
        load.wait()
    spread_weights(second_ref, spread_second)

    per_band = groups // heads
    chunk = per_band * sub
    lane_from = lax.broadcasted_iota(jnp.int32, (band, band), 0)
    lane_to = lax.broadcasted_iota(jnp.int32, (band, band), 1)
    wanted = (lane_from % chunk) // sub * size + lane_from // chunk * sub + lane_from % sub
    regroup = jnp.where(wanted == lane_to, 1.0, 0.0).astype(BF16)

    def regroup_half(half):
        top, length = cuts[half]
        for step in range(freq_count - 1):
            z_copy(partner(step), at_freq, half).wait_recv()
        for head in range(heads):
            pieces = [
                arrived[
                    source,
                    top : top + length,
                    piece * columns + head * chunk : piece * columns + (head + 1) * chunk,
                ]
                for source in range(freq_count)
                for piece in range(parts)
            ]
            shuffled[head, top : top + length] = ordered_dot(
                jnp.concatenate(pieces, axis=1), regroup
            )

    own_head, own_split = at_tm // splits, at_tm % splits

    def pair_copy(source, head, half):
        return pltpu.make_async_remote_copy(
            src_ref=pair_out.at[head, pl.ds(half * part, part)],
            dst_ref=pairs.at[source, pl.ds(half * part, part)],
            send_sem=kv_send.at[head * splits + half],
            recv_sem=kv_recv.at[source * splits + half],
            device_id={"tm": head * splits + own_split},
            device_id_type=MESH,
        )

    def forward_copy(source, step, half):
        return pltpu.make_async_remote_copy(
            src_ref=pairs.at[source, pl.ds(half * part, part)],
            dst_ref=pairs.at[source, pl.ds(half * part, part)],
            send_sem=forward_send.at[(source * splits + step) * splits + half],
            recv_sem=kv_recv.at[source * splits + half],
            device_id={"tm": own_head * splits + lax.rem(own_split + step, splits)},
            device_id_type=MESH,
        )

    def forward(source, half):
        for step in range(1, splits):
            forward_copy(source, step, half).start()

    def query_copy(source, head, split):
        target = head * splits + split
        return pltpu.make_async_remote_copy(
            src_ref=query_out.at[target],
            dst_ref=queries.at[source],
            send_sem=q_send.at[target],
            recv_sem=q_recv.at[source],
            device_id={"tm": target},
            device_id_type=MESH,
        )

    def project(head, half):
        top = half * part
        total = padded[head, 3 * margin + top : 3 * margin + top + part]
        total = total + convolve(shuffled, head, 2 * margin + top, part, spread_second)
        rounded = total.astype(BF16)
        resid[head, top : top + part] = rounded
        pair_out[head, top : top + part, 0:head_size] = ordered_dot(
            rounded, wk_ref[head]
        ).astype(BF16)
        pair_out[head, top : top + part, head_size:] = ordered_dot(
            rounded, wv_ref[head]
        ).astype(BF16)
        query_out[head * splits + half] = ordered_dot(rounded, wq_ref[head]).astype(BF16)

    for half in range(splits):
        regroup_half(half)

        def project_step(step, carry):
            head = lax.rem(own_head + step, heads)
            project(head, half)
            pair_copy(at_tm, head, half).start()
            query_copy(at_tm, head, half).start()
            return carry

        lax.fori_loop(1, heads, project_step, 0)
        project(own_head, half)
        top = half * part
        pairs[at_tm, top : top + part] = pair_out[own_head, top : top + part]
        forward(at_tm, half)

        @pl.when(own_split != half)
        def _():
            query_copy(at_tm, own_head, half).start()

    queries[at_tm] = query_out[at_tm]

    def att_copy(source, target):
        return pltpu.make_async_remote_copy(
            src_ref=att_out.at[target],
            dst_ref=att_in.at[source],
            send_sem=a_send.at[target],
            recv_sem=a_recv.at[source],
            device_id={"tm": target},
            device_id_type=MESH,
        )

    def pass_on(source):
        @pl.when(jnp.logical_and(own_split == source % splits, at_tm != source))
        def _():
            for half in range(splits):
                pair_copy(source, own_head, half).wait_recv()
                forward(source, half)

    def await_source(source):
        @pl.when(at_tm != source)
        def _():
            marks_copy(source, at_tm).wait_recv()
            query_copy(source, own_head, own_split).wait_recv()

        @pl.when(own_split != source % splits)
        def _():
            for half in range(splits):
                pair_copy(source, own_head, half).wait_recv()

    factor = math.log2(math.e) / math.sqrt(head_size)
    ahead = -(-BLOCK_MOST // LANES) * LANES
    contract = (((1,), (1,)), ((), ()))
    ready = 0
    for block in [b for i in range(splits) for b in range(i, tm_count, splits)]:
        needed = min(tm_count, block + 2)
        for source in range(ready, needed):
            pass_on(source)
        for source in range(ready, needed):
            await_source(source)
        ready = max(ready, needed)
        asked = queries[block]
        near = pairs[block]
        near_marks = marks[block][0:1].astype(F32)
        if block + 1 < tm_count:
            near = jnp.concatenate([near, pairs[block + 1, 0:ahead]], axis=0)
            near_marks = jnp.concatenate(
                [near_marks, marks[block + 1][0:1, 0:ahead].astype(F32)], axis=1
            )
        offset = pl.multiple_of(own_split * part, LANES)
        mine = marks[block, 0:1, pl.ds(offset, part)].astype(F32)
        mine = jnp.transpose(jnp.broadcast_to(mine, (part, part)))[:, 0:1]
        near_scores = lax.dot_general(
            asked, near[:, 0:head_size], contract, preferred_element_type=F32
        )
        near_scores = jnp.where(near_marks <= mine, near_scores, -1e30)
        peak = jnp.max(near_scores, axis=1, keepdims=True)
        if block > 0:
            far = pairs[0:block].reshape(block * count, 2 * head_size)
            far_scores = lax.dot_general(
                asked, far[:, 0:head_size], contract, preferred_element_type=F32
            )
            peak = jnp.maximum(peak, jnp.max(far_scores, axis=1, keepdims=True))
        weights = jnp.exp2((near_scores - peak) * factor)
        total = jnp.sum(weights, axis=1, keepdims=True)
        summed = ordered_dot(weights.astype(BF16), near[:, head_size:])
        if block > 0:
            weights = jnp.exp2((far_scores - peak) * factor)
            total = total + jnp.sum(weights, axis=1, keepdims=True)
            summed = summed + ordered_dot(weights.astype(BF16), far[:, head_size:])
        att_out[block] = (summed / total).astype(BF16)

        @pl.when(at_tm != block)
        def _():
            att_copy(at_tm, block).start()

    att_in[at_tm] = att_out[at_tm]
    for source in range(tm_count):

        @pl.when(at_tm != source)
        def _():
            att_copy(source, at_tm).wait_recv()

        head, split = source // splits, source % splits
        top = split * part
        added = ordered_dot(att_in[source], wo_ref[head])
        out_ref[top : top + part, head * band : (head + 1) * band] = (
            resid[head, top : top + part].astype(F32) + added
        ).astype(BF16)

    @pl.when(at_tm < tm_count - 1)
    def _():
        halo_copy().wait_send()

    for half in range(splits):
        for step in range(freq_count - 1):
            z_copy(at_freq, partner(step), half).wait_send()
        for step in range(1, heads):
            pair_copy(at_tm, lax.rem(own_head + step, heads), half).wait_send()
        for head in range(heads):
            for step in range(1, splits):
                forward_copy(head * splits + own_split, step, half).wait_send()
    for step in range(1, tm_count):
        target = lax.rem(at_tm + step, tm_count)
        marks_copy(at_tm, target).wait_send()
        query_copy(at_tm, target // splits, target % splits).wait_send()
        att_copy(at_tm, target).wait_send()


def per_device_fused(
    signal,
    conv_first,
    conv_second,
    shuffle,
    blocks,
    query_weight,
    key_weight,
    value_weight,
    out_weight,
):
    freq_count, tm_count = lax.axis_size("freq"), lax.axis_size("tm")
    count, width = signal.shape
    groups, taps, size, _ = conv_first.shape
    heads, band, head_size = query_weight.shape
    margin = taps - 1
    rows = count + 2 * margin
    part = count * heads // tm_count
    splits = tm_count // heads
    columns = groups * groups
    deep = heads * band * LANES // columns
    vmem = pl.BlockSpec(memory_space=pltpu.VMEM)
    hbm = pl.BlockSpec(memory_space=pl.ANY)
    dma = pltpu.SemaphoreType.DMA
    return pl.pallas_call(
        functools.partial(layer_kernel, freq_count, tm_count),
        out_shape=jax.ShapeDtypeStruct((count, width), BF16),
        in_specs=[vmem] * 3 + [hbm] * 6,
        out_specs=vmem,
        scratch_shapes=[
            pltpu.VMEM(conv_first.shape, BF16),
            pltpu.VMEM(conv_second.shape, BF16),
            pltpu.VMEM(query_weight.shape, BF16),
            pltpu.VMEM(key_weight.shape, BF16),
            pltpu.VMEM(value_weight.shape, BF16),
            pltpu.VMEM(out_weight.shape, BF16),
            pltpu.VMEM((freq_count, deep, LANES), BF16),
            pltpu.VMEM((8, count), jnp.int32),
            pltpu.VMEM((heads, rows + margin, band), F32),
            pltpu.VMEM((heads, taps, band, band), BF16),
            pltpu.VMEM((heads, taps, band, band), BF16),
            pltpu.VMEM((2 * margin, width), BF16),
            pltpu.VMEM((heads, rows, band), BF16),
            pltpu.VMEM((freq_count, rows, columns), BF16),
            pltpu.VMEM((freq_count, rows, columns), BF16),
            pltpu.VMEM((heads, rows, band), F32),
            pltpu.VMEM((heads, count, band), BF16),
            pltpu.VMEM((heads, count, 2 * head_size), BF16),
            pltpu.VMEM((tm_count, part, head_size), BF16),
            pltpu.VMEM((tm_count, count, 2 * head_size), BF16),
            pltpu.VMEM((tm_count, part, head_size), BF16),
            pltpu.VMEM((tm_count, 8, count), jnp.int32),
            pltpu.VMEM((tm_count, part, head_size), BF16),
            pltpu.VMEM((tm_count, part, head_size), BF16),
            dma((2,)),
            dma((freq_count * splits,)),
            dma((freq_count * splits,)),
        ]
        + [dma((tm_count,))] * 2
        + [dma((tm_count,)), dma((tm_count * splits,))]
        + [dma((tm_count,))] * 4
        + [dma((tm_count * splits * splits,)), dma((6,))],
        compiler_params=pltpu.CompilerParams(
            collective_id=0, has_side_effects=True, vmem_limit_bytes=56 * 1024 * 1024
        ),
        cost_estimate=pl.CostEstimate(
            flops=10**10, bytes_accessed=8 * 10**6, transcendentals=2 * 10**6
        ),
    )(
        signal,
        shuffle[None, :],
        blocks[None, :],
        conv_first,
        conv_second,
        query_weight,
        key_weight,
        value_weight,
        out_weight,
    )


def fits_fused(signal, conv_first, query_weight):
    tm_count = lax.axis_size("tm")
    count = signal.shape[0]
    groups, taps, size, _ = conv_first.shape
    heads, band, head_size = query_weight.shape
    return (
        tm_count % heads == 0
        and (count * heads) % (LANES * tm_count) == 0
        and (groups * groups) % LANES == 0
        and LANES % groups == 0
        and heads % (groups * groups // LANES) == 0
        and lax.axis_size("freq") % 2 == 0
        and groups % heads == 0
        and heads * band == signal.shape[1]
        and (taps - 1) % 8 == 0
        and LANES % size == 0
        and band % LANES == 0
        and head_size % LANES == 0
        and size % 16 == 0
    )


def passed_along(block, axis, distance):
    devices = range(lax.axis_size(axis))
    route = [(i - distance, i) for i in devices if i - distance in devices]
    return lax.ppermute(block, axis, route)


def conv_local(padded, weights, length, form):
    margin = weights.shape[1] - 1
    result = None
    for offset in range(weights.shape[1]):
        term = jnp.einsum(
            form,
            padded[margin - offset : margin - offset + length],
            weights[:, offset],
            preferred_element_type=jnp.float32,
        )
        result = term if result is None else result + term
    return result


def split_range(count, width):
    return [(offset, min(offset + width, count)) for offset in range(0, count, width)]


def update_tile(state, query_part, query_marks, key_part, value_part, key_marks):
    peak, total, summed = state
    scale = 1.0 / math.sqrt(query_part.shape[2])
    scores = (
        jnp.einsum("qhd,khd->hqk", query_part, key_part, preferred_element_type=jnp.float32) * scale
    )
    seen = key_marks[None, None, :] <= query_marks[None, :, None]
    masked = jnp.where(seen, scores, jnp.float32(-1e30))
    new_peak = jnp.maximum(peak, jnp.max(masked, axis=2))
    weights = jnp.where(seen, jnp.exp(masked - new_peak[:, :, None]), jnp.float32(0.0))
    factor = jnp.exp(peak - new_peak)
    total = total * factor + jnp.sum(weights, axis=2)
    summed = summed * factor[:, :, None] + jnp.einsum(
        "hqk,khd->hqd", weights.astype(jnp.bfloat16), value_part, preferred_element_type=jnp.float32
    )
    return (new_peak, total, summed)


def unchanged(state, *others):
    return state


def make_fold(queries, query_marks):
    count = queries.shape[0]
    query_cuts = split_range(count, max(1, count // 2))

    def fold(carry, piece, start):
        key_rows, value_rows, key_marks = piece
        key_cuts = split_range(key_rows.shape[0], max(1, count // 2))
        peak, total, summed = carry
        results = []
        for top_row, end_row in query_cuts:
            state = (
                peak[:, top_row:end_row],
                total[:, top_row:end_row],
                summed[:, top_row:end_row],
            )
            for key_top, key_end in key_cuts:
                needed = jnp.min(key_marks[key_top:key_end]) <= jnp.max(
                    query_marks[top_row:end_row]
                )
                state = lax.cond(
                    needed,
                    update_tile,
                    unchanged,
                    state,
                    queries[top_row:end_row],
                    query_marks[top_row:end_row],
                    key_rows[key_top:key_end],
                    value_rows[key_top:key_end],
                    key_marks[key_top:key_end],
                )
            results.append(state)
        return tuple(
            (jnp.concatenate([entry[member] for entry in results], axis=1) for member in range(3))
        )

    return fold


def start_state(heads_here, count, head_size):
    return (
        jnp.full((heads_here, count), -1e30, jnp.float32),
        jnp.zeros((heads_here, count), jnp.float32),
        jnp.zeros((heads_here, count, head_size), jnp.float32),
    )


def finish(state):
    peak, total, summed = state
    return jnp.transpose(summed / total[:, :, None], (1, 0, 2)).astype(jnp.bfloat16)


def per_device_plain(
    signal,
    conv_first,
    conv_second,
    shuffle,
    blocks,
    query_weight,
    key_weight,
    value_weight,
    out_weight,
):
    count, width = signal.shape
    groups_here = conv_first.shape[0]
    group_size = conv_first.shape[2]
    margin = conv_first.shape[1] - 1
    local = signal.reshape(count, groups_here, group_size)
    selector = (shuffle[None, :] == jnp.arange(group_size, dtype=jnp.int32)[:, None]).astype(
        jnp.bfloat16
    )
    before = passed_along(local[count - 2 * margin :], "tm", 1)
    padded = jnp.concatenate([before, local], axis=0)
    first = jax.nn.silu(conv_local(padded, conv_first, count + margin, "tgi,gio->tgo")).astype(
        jnp.bfloat16
    )
    permuted = jnp.einsum(
        "tgj,jk->tgk", first, selector, preferred_element_type=jnp.float32
    ).astype(jnp.bfloat16)
    shuffled = lax.all_to_all(permuted, "freq", split_axis=2, concat_axis=1, tiled=True)
    second = conv_local(shuffled, conv_second, count, "tgk,kgo->tko")
    resid = (signal.astype(jnp.float32) + second.reshape(count, width)).astype(jnp.bfloat16)
    heads_here, band, head_size = query_weight.shape
    bands = resid.reshape(count, heads_here, band)
    queries = jnp.einsum(
        "thc,hcd->thd", bands, query_weight, preferred_element_type=jnp.float32
    ).astype(jnp.bfloat16)
    keys = jnp.einsum("thc,hcd->thd", bands, key_weight, preferred_element_type=jnp.float32).astype(
        jnp.bfloat16
    )
    values = jnp.einsum(
        "thc,hcd->thd", bands, value_weight, preferred_element_type=jnp.float32
    ).astype(jnp.bfloat16)
    initial = start_state(heads_here, count, head_size)
    fold = make_fold(queries, blocks)
    state = fold(
        initial,
        (
            lax.all_gather(keys, "tm", axis=0, tiled=True),
            lax.all_gather(values, "tm", axis=0, tiled=True),
            lax.all_gather(blocks, "tm", axis=0, tiled=True),
        ),
        jnp.int32(0),
    )
    attended = finish(state)
    added = jnp.einsum("thd,hdc->thc", attended, out_weight, preferred_element_type=jnp.float32)
    return (resid.astype(jnp.float32) + added.reshape(count, width)).astype(jnp.bfloat16)


def per_device(*args):
    if fits_fused(args[0], args[1], args[5]):
        return per_device_fused(*args)
    return per_device_plain(*args)


def solution(mesh):
    in_specs = (
        P("tm", "freq"),
        P("freq", None, None, None),
        P("freq", None, None, None),
        P(),
        P("tm"),
        P("freq", None, None),
        P("freq", None, None),
        P("freq", None, None),
        P("freq", None, None),
    )
    out_specs = P("tm", "freq")
    return jax.shard_map(
        per_device, mesh=mesh, in_specs=in_specs, out_specs=out_specs, check_vma=False
    )
```

```python
import functools
import math

import jax
import jax.numpy as jnp
from jax import lax
from jax.experimental import pallas as pl
from jax.experimental.pallas import tpu as pltpu
from jax.sharding import PartitionSpec as P

MESH = pl.DeviceIdType.MESH
BLOCK_MOST = 64
LANES = 128
F32 = jnp.float32
BF16 = jnp.bfloat16


def ordered_dot(a, b):
    return jnp.dot(a, b, preferred_element_type=F32)


def spread_weights(weights_ref, spread_ref):
    spread_ref[...] = jnp.zeros_like(spread_ref)
    groups, taps, size, _ = weights_ref.shape
    per_band = spread_ref.shape[2] // size
    per_tile = LANES // size
    for group in range(groups):
        place = group % per_band
        tile, slot = place // per_tile, place % per_tile
        block = weights_ref[group]
        parts = [block if i == slot else jnp.zeros_like(block) for i in range(per_tile)]
        spread_ref[
            group // per_band,
            :,
            place * size : (place + 1) * size,
            tile * LANES : (tile + 1) * LANES,
        ] = jnp.concatenate(parts, axis=2)


def layer_kernel(
    freq_count,
    tm_count,
    signal_ref,
    shuffle_ref,
    blocks_ref,
    first_hbm,
    second_hbm,
    wq_hbm,
    wk_hbm,
    wv_hbm,
    wo_hbm,
    out_ref,
    first_ref,
    second_ref,
    wq_ref,
    wk_ref,
    wv_ref,
    wo_ref,
    picks,
    marks_ref,
    padded,
    spread_first,
    spread_second,
    halo,
    first,
    sending,
    arrived,
    shuffled,
    resid,
    pair_out,
    query_out,
    pairs,
    queries,
    marks,
    att_out,
    att_in,
    halo_sem,
    z_send,
    z_recv,
    b_send,
    b_recv,
    kv_send,
    kv_recv,
    q_send,
    q_recv,
    a_send,
    a_recv,
    forward_send,
    load_sem,
):
    at_freq, at_tm = lax.axis_index("freq"), lax.axis_index("tm")
    count = signal_ref.shape[0]
    heads, band, head_size = wq_ref.shape
    taps = first_ref.shape[1]
    groups = first_ref.shape[0]
    margin = taps - 1
    rows = count + 2 * margin
    splits = tm_count // heads
    part = count // splits

    barrier = pltpu.get_barrier_semaphore()
    for step in range(1, freq_count):
        pl.semaphore_signal(
            barrier,
            inc=1,
            device_id={"freq": lax.rem(at_freq + step, freq_count)},
            device_id_type=MESH,
        )
    for step in range(1, tm_count):
        pl.semaphore_signal(
            barrier,
            inc=1,
            device_id={"tm": lax.rem(at_tm + step, tm_count)},
            device_id_type=MESH,
        )
    loads = [
        pltpu.make_async_copy(whole, local, load_sem.at[i])
        for i, (whole, local) in enumerate(
            (
                (first_hbm, first_ref),
                (second_hbm, second_ref),
                (wq_hbm, wq_ref),
                (wk_hbm, wk_ref),
                (wv_hbm, wv_ref),
                (wo_hbm, wo_ref),
            )
        )
    ]
    loads[0].start()
    marks_ref[...] = jnp.broadcast_to(blocks_ref[...], marks_ref.shape)
    for head in range(heads):
        padded[head, 0 : 3 * margin] = jnp.zeros((3 * margin, band), F32)
        padded[head, 3 * margin :] = signal_ref[:, head * band : (head + 1) * band].astype(F32)

    columns = picks.shape[2]
    size = first_ref.shape[2]
    sub = columns // groups
    parts = groups // sub
    part_heads = heads // parts
    deep = part_heads * band
    total_lanes = freq_count * columns
    channel = shuffle_ref.shape[1]
    spread = jnp.where(
        lax.broadcasted_iota(jnp.int32, (channel, total_lanes), 1) // sub
        == lax.broadcasted_iota(jnp.int32, (channel, total_lanes), 0),
        1.0,
        0.0,
    ).astype(BF16)
    taken = jnp.broadcast_to(shuffle_ref[...].astype(F32), (16, channel)).astype(BF16)
    lane = lax.broadcasted_iota(jnp.int32, (16, total_lanes), 1)
    taken = ordered_dot(taken, spread) + (lane % sub * size).astype(F32)
    row_ids = lax.broadcasted_iota(jnp.int32, (deep, columns), 0).astype(F32)
    for target in range(freq_count):
        source = taken[0:1, target * columns : (target + 1) * columns]
        picks[target] = jnp.where(row_ids == source, 1.0, 0.0).astype(BF16)
    pl.semaphore_wait(barrier, freq_count + tm_count - 2)

    def halo_copy():
        return pltpu.make_async_remote_copy(
            src_ref=signal_ref.at[pl.ds(count - 2 * margin, 2 * margin)],
            dst_ref=halo,
            send_sem=halo_sem.at[0],
            recv_sem=halo_sem.at[1],
            device_id={"tm": lax.rem(at_tm + 1, tm_count)},
            device_id_type=MESH,
        )

    @pl.when(at_tm < tm_count - 1)
    def _():
        halo_copy().start()

    def marks_copy(source, target):
        return pltpu.make_async_remote_copy(
            src_ref=marks_ref,
            dst_ref=marks.at[source],
            send_sem=b_send.at[target],
            recv_sem=b_recv.at[source],
            device_id={"tm": target},
            device_id_type=MESH,
        )

    for step in range(1, tm_count):
        marks_copy(at_tm, lax.rem(at_tm + step, tm_count)).start()
    marks[at_tm] = marks_ref[...]
    loads[0].wait()
    for load in loads[1:]:
        load.start()
    spread_weights(first_ref, spread_first)

    @pl.when(at_tm > 0)
    def _():
        halo_copy().wait_recv()
        for head in range(heads):
            padded[head, margin : 3 * margin] = halo[:, head * band : (head + 1) * band].astype(F32)

    def convolve(source, head, top, length, spread_ref):
        windows = [source[head, top - tap : top - tap + length] for tap in range(taps)]
        windows = jnp.concatenate([window.astype(BF16) for window in windows], axis=1)
        return ordered_dot(windows, spread_ref[head].reshape(taps * band, band))

    cuts = [(0, 2 * margin + part)] + [
        (2 * margin + i * part, part) for i in range(1, splits)
    ]

    def z_copy(source, target, half):
        top, length = cuts[half]
        return pltpu.make_async_remote_copy(
            src_ref=sending.at[target, pl.ds(top, length)],
            dst_ref=arrived.at[source, pl.ds(top, length)],
            send_sem=z_send.at[target * splits + half],
            recv_sem=z_recv.at[source * splits + half],
            device_id={"freq": target},
            device_id_type=MESH,
        )

    def shuffle_for(target, half, out):
        top, length = cuts[half]
        for piece in range(parts):
            held = [
                first[piece * part_heads + i, top : top + length] for i in range(part_heads)
            ]
            out[target, top : top + length, piece * columns : (piece + 1) * columns] = ordered_dot(
                jnp.concatenate(held, axis=1), picks[target]
            ).astype(BF16)

    def partner(step):
        chips = freq_count // 2
        chip = lax.rem(at_freq // 2 + step // 2 + 1, chips)
        return chip * 2 + lax.rem(at_freq % 2 + 1 + step % 2, 2)

    for half in range(splits):
        top, length = cuts[half]

        def convolve_first(head, carry):
            total = convolve(padded, head, margin + top, length, spread_first)
            first[head, top : top + length] = (total / (1.0 + jnp.exp(-total))).astype(BF16)
            return carry

        lax.fori_loop(0, heads, convolve_first, 0)

        def shuffle_step(step, carry):
            target = partner(step)
            shuffle_for(target, half, sending)
            z_copy(at_freq, target, half).start()
            return carry

        lax.fori_loop(0, freq_count - 1, shuffle_step, 0)
    for half in range(splits):
        shuffle_for(at_freq, half, arrived)
    for load in loads[1:]:
        load.wait()
    spread_weights(second_ref, spread_second)

    per_band = groups // heads
    chunk = per_band * sub
    lane_from = lax.broadcasted_iota(jnp.int32, (band, band), 0)
    lane_to = lax.broadcasted_iota(jnp.int32, (band, band), 1)
    wanted = (lane_from % chunk) // sub * size + lane_from // chunk * sub + lane_from % sub
    regroup = jnp.where(wanted == lane_to, 1.0, 0.0).astype(BF16)

    def regroup_half(half):
        top, length = cuts[half]
        for step in range(freq_count - 1):
            z_copy(partner(step), at_freq, half).wait_recv()
        for head in range(heads):
            pieces = [
                arrived[
                    source,
                    top : top + length,
                    piece * columns + head * chunk : piece * columns + (head + 1) * chunk,
                ]
                for source in range(freq_count)
                for piece in range(parts)
            ]
            shuffled[head, top : top + length] = ordered_dot(
                jnp.concatenate(pieces, axis=1), regroup
            )

    own_head, own_split = at_tm // splits, at_tm % splits

    def pair_copy(source, head, half):
        return pltpu.make_async_remote_copy(
            src_ref=pair_out.at[head, pl.ds(half * part, part)],
            dst_ref=pairs.at[source, pl.ds(half * part, part)],
            send_sem=kv_send.at[head * splits + half],
            recv_sem=kv_recv.at[source * splits + half],
            device_id={"tm": head * splits + own_split},
            device_id_type=MESH,
        )

    def forward_copy(source, step, half):
        return pltpu.make_async_remote_copy(
            src_ref=pairs.at[source, pl.ds(half * part, part)],
            dst_ref=pairs.at[source, pl.ds(half * part, part)],
            send_sem=forward_send.at[(source * splits + step) * splits + half],
            recv_sem=kv_recv.at[source * splits + half],
            device_id={"tm": own_head * splits + lax.rem(own_split + step, splits)},
            device_id_type=MESH,
        )

    def forward(source, half):
        for step in range(1, splits):
            forward_copy(source, step, half).start()

    def query_copy(source, head, split):
        target = head * splits + split
        return pltpu.make_async_remote_copy(
            src_ref=query_out.at[target],
            dst_ref=queries.at[source],
            send_sem=q_send.at[target],
            recv_sem=q_recv.at[source],
            device_id={"tm": target},
            device_id_type=MESH,
        )

    def project(head, half):
        top = half * part
        total = padded[head, 3 * margin + top : 3 * margin + top + part]
        total = total + convolve(shuffled, head, 2 * margin + top, part, spread_second)
        rounded = total.astype(BF16)
        resid[head, top : top + part] = rounded
        pair_out[head, top : top + part, 0:head_size] = ordered_dot(
            rounded, wk_ref[head]
        ).astype(BF16)
        pair_out[head, top : top + part, head_size:] = ordered_dot(
            rounded, wv_ref[head]
        ).astype(BF16)
        query_out[head * splits + half] = ordered_dot(rounded, wq_ref[head]).astype(BF16)

    for half in range(splits):
        regroup_half(half)

        def project_step(step, carry):
            head = lax.rem(own_head + step, heads)
            project(head, half)
            pair_copy(at_tm, head, half).start()
            query_copy(at_tm, head, half).start()
            return carry

        lax.fori_loop(1, heads, project_step, 0)
        project(own_head, half)
        top = half * part
        pairs[at_tm, top : top + part] = pair_out[own_head, top : top + part]
        forward(at_tm, half)

        @pl.when(own_split != half)
        def _():
            query_copy(at_tm, own_head, half).start()

    queries[at_tm] = query_out[at_tm]

    def att_copy(source, target):
        return pltpu.make_async_remote_copy(
            src_ref=att_out.at[target],
            dst_ref=att_in.at[source],
            send_sem=a_send.at[target],
            recv_sem=a_recv.at[source],
            device_id={"tm": target},
            device_id_type=MESH,
        )

    def pass_on(source, half):
        @pl.when(jnp.logical_and(own_split == source % splits, at_tm != source))
        def _():
            pair_copy(source, own_head, half).wait_recv()
            forward(source, half)

    def await_source(source):
        @pl.when(at_tm != source)
        def _():
            marks_copy(source, at_tm).wait_recv()
            query_copy(source, own_head, own_split).wait_recv()

        @pl.when(own_split != source % splits)
        def _():
            for half in range(splits):
                pair_copy(source, own_head, half).wait_recv()

    factor = math.log2(math.e) / math.sqrt(head_size)
    ahead = -(-BLOCK_MOST // LANES) * LANES
    contract = (((1,), (1,)), ((), ()))
    for half in range(splits):
        for source in range(tm_count):
            pass_on(source, half)
    await_source(0)
    for block in range(tm_count):
        if block + 1 < tm_count:
            await_source(block + 1)
        asked = queries[block]
        near = pairs[block]
        near_marks = marks[block][0:1].astype(F32)
        if block + 1 < tm_count:
            near = jnp.concatenate([near, pairs[block + 1, 0:ahead]], axis=0)
            near_marks = jnp.concatenate(
                [near_marks, marks[block + 1][0:1, 0:ahead].astype(F32)], axis=1
            )
        offset = pl.multiple_of(own_split * part, LANES)
        mine = marks[block, 0:1, pl.ds(offset, part)].astype(F32)
        mine = jnp.transpose(jnp.broadcast_to(mine, (part, part)))[:, 0:1]
        near_scores = lax.dot_general(
            asked, near[:, 0:head_size], contract, preferred_element_type=F32
        )
        near_scores = jnp.where(near_marks <= mine, near_scores, -1e30)
        peak = jnp.max(near_scores, axis=1, keepdims=True)
        if block > 0:
            far = pairs[0:block].reshape(block * count, 2 * head_size)
            far_scores = lax.dot_general(
                asked, far[:, 0:head_size], contract, preferred_element_type=F32
            )
            peak = jnp.maximum(peak, jnp.max(far_scores, axis=1, keepdims=True))
        weights = jnp.exp2((near_scores - peak) * factor)
        total = jnp.sum(weights, axis=1, keepdims=True)
        summed = ordered_dot(weights.astype(BF16), near[:, head_size:])
        if block > 0:
            weights = jnp.exp2((far_scores - peak) * factor)
            total = total + jnp.sum(weights, axis=1, keepdims=True)
            summed = summed + ordered_dot(weights.astype(BF16), far[:, head_size:])
        att_out[block] = (summed / total).astype(BF16)

        @pl.when(at_tm != block)
        def _():
            att_copy(at_tm, block).start()

    att_in[at_tm] = att_out[at_tm]
    for source in range(tm_count):

        @pl.when(at_tm != source)
        def _():
            att_copy(source, at_tm).wait_recv()

        head, split = source // splits, source % splits
        top = split * part
        added = ordered_dot(att_in[source], wo_ref[head])
        out_ref[top : top + part, head * band : (head + 1) * band] = (
            resid[head, top : top + part].astype(F32) + added
        ).astype(BF16)

    @pl.when(at_tm < tm_count - 1)
    def _():
        halo_copy().wait_send()

    for half in range(splits):
        for step in range(freq_count - 1):
            z_copy(at_freq, partner(step), half).wait_send()
        for step in range(1, heads):
            pair_copy(at_tm, lax.rem(own_head + step, heads), half).wait_send()
        for head in range(heads):
            for step in range(1, splits):
                forward_copy(head * splits + own_split, step, half).wait_send()
    for step in range(1, tm_count):
        target = lax.rem(at_tm + step, tm_count)
        marks_copy(at_tm, target).wait_send()
        query_copy(at_tm, target // splits, target % splits).wait_send()
        att_copy(at_tm, target).wait_send()


def per_device_fused(
    signal,
    conv_first,
    conv_second,
    shuffle,
    blocks,
    query_weight,
    key_weight,
    value_weight,
    out_weight,
):
    freq_count, tm_count = lax.axis_size("freq"), lax.axis_size("tm")
    count, width = signal.shape
    groups, taps, size, _ = conv_first.shape
    heads, band, head_size = query_weight.shape
    margin = taps - 1
    rows = count + 2 * margin
    part = count * heads // tm_count
    splits = tm_count // heads
    columns = groups * groups
    deep = heads * band * LANES // columns
    vmem = pl.BlockSpec(memory_space=pltpu.VMEM)
    hbm = pl.BlockSpec(memory_space=pl.ANY)
    dma = pltpu.SemaphoreType.DMA
    return pl.pallas_call(
        functools.partial(layer_kernel, freq_count, tm_count),
        out_shape=jax.ShapeDtypeStruct((count, width), BF16),
        in_specs=[vmem] * 3 + [hbm] * 6,
        out_specs=vmem,
        scratch_shapes=[
            pltpu.VMEM(conv_first.shape, BF16),
            pltpu.VMEM(conv_second.shape, BF16),
            pltpu.VMEM(query_weight.shape, BF16),
            pltpu.VMEM(key_weight.shape, BF16),
            pltpu.VMEM(value_weight.shape, BF16),
            pltpu.VMEM(out_weight.shape, BF16),
            pltpu.VMEM((freq_count, deep, LANES), BF16),
            pltpu.VMEM((8, count), jnp.int32),
            pltpu.VMEM((heads, rows + margin, band), F32),
            pltpu.VMEM((heads, taps, band, band), BF16),
            pltpu.VMEM((heads, taps, band, band), BF16),
            pltpu.VMEM((2 * margin, width), BF16),
            pltpu.VMEM((heads, rows, band), BF16),
            pltpu.VMEM((freq_count, rows, columns), BF16),
            pltpu.VMEM((freq_count, rows, columns), BF16),
            pltpu.VMEM((heads, rows, band), F32),
            pltpu.VMEM((heads, count, band), BF16),
            pltpu.VMEM((heads, count, 2 * head_size), BF16),
            pltpu.VMEM((tm_count, part, head_size), BF16),
            pltpu.VMEM((tm_count, count, 2 * head_size), BF16),
            pltpu.VMEM((tm_count, part, head_size), BF16),
            pltpu.VMEM((tm_count, 8, count), jnp.int32),
            pltpu.VMEM((tm_count, part, head_size), BF16),
            pltpu.VMEM((tm_count, part, head_size), BF16),
            dma((2,)),
            dma((freq_count * splits,)),
            dma((freq_count * splits,)),
        ]
        + [dma((tm_count,))] * 2
        + [dma((tm_count,)), dma((tm_count * splits,))]
        + [dma((tm_count,))] * 4
        + [dma((tm_count * splits * splits,)), dma((6,))],
        compiler_params=pltpu.CompilerParams(
            collective_id=0, has_side_effects=True, vmem_limit_bytes=56 * 1024 * 1024
        ),
        cost_estimate=pl.CostEstimate(
            flops=10**10, bytes_accessed=8 * 10**6, transcendentals=2 * 10**6
        ),
    )(
        signal,
        shuffle[None, :],
        blocks[None, :],
        conv_first,
        conv_second,
        query_weight,
        key_weight,
        value_weight,
        out_weight,
    )


def fits_fused(signal, conv_first, query_weight):
    tm_count = lax.axis_size("tm")
    count = signal.shape[0]
    groups, taps, size, _ = conv_first.shape
    heads, band, head_size = query_weight.shape
    return (
        tm_count % heads == 0
        and (count * heads) % (LANES * tm_count) == 0
        and (groups * groups) % LANES == 0
        and LANES % groups == 0
        and heads % (groups * groups // LANES) == 0
        and lax.axis_size("freq") % 2 == 0
        and groups % heads == 0
        and heads * band == signal.shape[1]
        and (taps - 1) % 8 == 0
        and LANES % size == 0
        and band % LANES == 0
        and head_size % LANES == 0
        and size % 16 == 0
    )


def passed_along(block, axis, distance):
    devices = range(lax.axis_size(axis))
    route = [(i - distance, i) for i in devices if i - distance in devices]
    return lax.ppermute(block, axis, route)


def conv_local(padded, weights, length, form):
    margin = weights.shape[1] - 1
    result = None
    for offset in range(weights.shape[1]):
        term = jnp.einsum(
            form,
            padded[margin - offset : margin - offset + length],
            weights[:, offset],
            preferred_element_type=jnp.float32,
        )
        result = term if result is None else result + term
    return result


def split_range(count, width):
    return [(offset, min(offset + width, count)) for offset in range(0, count, width)]


def update_tile(state, query_part, query_marks, key_part, value_part, key_marks):
    peak, total, summed = state
    scale = 1.0 / math.sqrt(query_part.shape[2])
    scores = (
        jnp.einsum("qhd,khd->hqk", query_part, key_part, preferred_element_type=jnp.float32) * scale
    )
    seen = key_marks[None, None, :] <= query_marks[None, :, None]
    masked = jnp.where(seen, scores, jnp.float32(-1e30))
    new_peak = jnp.maximum(peak, jnp.max(masked, axis=2))
    weights = jnp.where(seen, jnp.exp(masked - new_peak[:, :, None]), jnp.float32(0.0))
    factor = jnp.exp(peak - new_peak)
    total = total * factor + jnp.sum(weights, axis=2)
    summed = summed * factor[:, :, None] + jnp.einsum(
        "hqk,khd->hqd", weights.astype(jnp.bfloat16), value_part, preferred_element_type=jnp.float32
    )
    return (new_peak, total, summed)


def unchanged(state, *others):
    return state


def make_fold(queries, query_marks):
    count = queries.shape[0]
    query_cuts = split_range(count, max(1, count // 2))

    def fold(carry, piece, start):
        key_rows, value_rows, key_marks = piece
        key_cuts = split_range(key_rows.shape[0], max(1, count // 2))
        peak, total, summed = carry
        results = []
        for top_row, end_row in query_cuts:
            state = (
                peak[:, top_row:end_row],
                total[:, top_row:end_row],
                summed[:, top_row:end_row],
            )
            for key_top, key_end in key_cuts:
                needed = jnp.min(key_marks[key_top:key_end]) <= jnp.max(
                    query_marks[top_row:end_row]
                )
                state = lax.cond(
                    needed,
                    update_tile,
                    unchanged,
                    state,
                    queries[top_row:end_row],
                    query_marks[top_row:end_row],
                    key_rows[key_top:key_end],
                    value_rows[key_top:key_end],
                    key_marks[key_top:key_end],
                )
            results.append(state)
        return tuple(
            (jnp.concatenate([entry[member] for entry in results], axis=1) for member in range(3))
        )

    return fold


def start_state(heads_here, count, head_size):
    return (
        jnp.full((heads_here, count), -1e30, jnp.float32),
        jnp.zeros((heads_here, count), jnp.float32),
        jnp.zeros((heads_here, count, head_size), jnp.float32),
    )


def finish(state):
    peak, total, summed = state
    return jnp.transpose(summed / total[:, :, None], (1, 0, 2)).astype(jnp.bfloat16)


def per_device_plain(
    signal,
    conv_first,
    conv_second,
    shuffle,
    blocks,
    query_weight,
    key_weight,
    value_weight,
    out_weight,
):
    count, width = signal.shape
    groups_here = conv_first.shape[0]
    group_size = conv_first.shape[2]
    margin = conv_first.shape[1] - 1
    local = signal.reshape(count, groups_here, group_size)
    selector = (shuffle[None, :] == jnp.arange(group_size, dtype=jnp.int32)[:, None]).astype(
        jnp.bfloat16
    )
    before = passed_along(local[count - 2 * margin :], "tm", 1)
    padded = jnp.concatenate([before, local], axis=0)
    first = jax.nn.silu(conv_local(padded, conv_first, count + margin, "tgi,gio->tgo")).astype(
        jnp.bfloat16
    )
    permuted = jnp.einsum(
        "tgj,jk->tgk", first, selector, preferred_element_type=jnp.float32
    ).astype(jnp.bfloat16)
    shuffled = lax.all_to_all(permuted, "freq", split_axis=2, concat_axis=1, tiled=True)
    second = conv_local(shuffled, conv_second, count, "tgk,kgo->tko")
    resid = (signal.astype(jnp.float32) + second.reshape(count, width)).astype(jnp.bfloat16)
    heads_here, band, head_size = query_weight.shape
    bands = resid.reshape(count, heads_here, band)
    queries = jnp.einsum(
        "thc,hcd->thd", bands, query_weight, preferred_element_type=jnp.float32
    ).astype(jnp.bfloat16)
    keys = jnp.einsum("thc,hcd->thd", bands, key_weight, preferred_element_type=jnp.float32).astype(
        jnp.bfloat16
    )
    values = jnp.einsum(
        "thc,hcd->thd", bands, value_weight, preferred_element_type=jnp.float32
    ).astype(jnp.bfloat16)
    initial = start_state(heads_here, count, head_size)
    fold = make_fold(queries, blocks)
    state = fold(
        initial,
        (
            lax.all_gather(keys, "tm", axis=0, tiled=True),
            lax.all_gather(values, "tm", axis=0, tiled=True),
            lax.all_gather(blocks, "tm", axis=0, tiled=True),
        ),
        jnp.int32(0),
    )
    attended = finish(state)
    added = jnp.einsum("thd,hdc->thc", attended, out_weight, preferred_element_type=jnp.float32)
    return (resid.astype(jnp.float32) + added.reshape(count, width)).astype(jnp.bfloat16)


def per_device(*args):
    if fits_fused(args[0], args[1], args[5]):
        return per_device_fused(*args)
    return per_device_plain(*args)


def solution(mesh):
    in_specs = (
        P("tm", "freq"),
        P("freq", None, None, None),
        P("freq", None, None, None),
        P(),
        P("tm"),
        P("freq", None, None),
        P("freq", None, None),
        P("freq", None, None),
        P("freq", None, None),
    )
    out_specs = P("tm", "freq")
    return jax.shard_map(
        per_device, mesh=mesh, in_specs=in_specs, out_specs=out_specs, check_vma=False
    )
```

```python
import functools
import math

import jax
import jax.numpy as jnp
from jax import lax
from jax.experimental import pallas as pl
from jax.experimental.pallas import tpu as pltpu
from jax.sharding import PartitionSpec as P

MESH = pl.DeviceIdType.MESH
BLOCK_MOST = 64
LANES = 128
F32 = jnp.float32
BF16 = jnp.bfloat16


def ordered_dot(a, b):
    return jnp.dot(a, b, preferred_element_type=F32)


def spread_weights(weights_ref, spread_ref):
    spread_ref[...] = jnp.zeros_like(spread_ref)
    groups, taps, size, _ = weights_ref.shape
    per_band = spread_ref.shape[2] // size
    per_tile = LANES // size
    for group in range(groups):
        place = group % per_band
        tile, slot = place // per_tile, place % per_tile
        block = weights_ref[group]
        parts = [block if i == slot else jnp.zeros_like(block) for i in range(per_tile)]
        spread_ref[
            group // per_band,
            :,
            place * size : (place + 1) * size,
            tile * LANES : (tile + 1) * LANES,
        ] = jnp.concatenate(parts, axis=2)


def layer_kernel(
    freq_count,
    tm_count,
    signal_ref,
    shuffle_ref,
    blocks_ref,
    first_hbm,
    second_hbm,
    wq_hbm,
    wk_hbm,
    wv_hbm,
    wo_hbm,
    out_ref,
    first_ref,
    second_ref,
    wq_ref,
    wk_ref,
    wv_ref,
    wo_ref,
    picks,
    marks_ref,
    padded,
    spread_first,
    spread_second,
    halo,
    first,
    sending,
    arrived,
    shuffled,
    resid,
    pair_out,
    query_out,
    pairs,
    queries,
    marks,
    att_out,
    att_in,
    halo_sem,
    z_send,
    z_recv,
    b_send,
    b_recv,
    kv_send,
    kv_recv,
    q_send,
    q_recv,
    a_send,
    a_recv,
    forward_send,
    load_sem,
):
    at_freq, at_tm = lax.axis_index("freq"), lax.axis_index("tm")
    count = signal_ref.shape[0]
    heads, band, head_size = wq_ref.shape
    taps = first_ref.shape[1]
    groups = first_ref.shape[0]
    margin = taps - 1
    rows = count + 2 * margin
    splits = tm_count // heads
    part = count // splits

    barrier = pltpu.get_barrier_semaphore()
    for step in range(1, freq_count):
        pl.semaphore_signal(
            barrier,
            inc=1,
            device_id={"freq": lax.rem(at_freq + step, freq_count)},
            device_id_type=MESH,
        )
    for step in range(1, tm_count):
        pl.semaphore_signal(
            barrier,
            inc=1,
            device_id={"tm": lax.rem(at_tm + step, tm_count)},
            device_id_type=MESH,
        )
    loads = [
        pltpu.make_async_copy(whole, local, load_sem.at[i])
        for i, (whole, local) in enumerate(
            (
                (first_hbm, first_ref),
                (second_hbm, second_ref),
                (wq_hbm, wq_ref),
                (wk_hbm, wk_ref),
                (wv_hbm, wv_ref),
                (wo_hbm, wo_ref),
            )
        )
    ]
    loads[0].start()
    marks_ref[...] = jnp.broadcast_to(blocks_ref[...], marks_ref.shape)
    for head in range(heads):
        padded[head, 0 : 3 * margin] = jnp.zeros((3 * margin, band), F32)
        padded[head, 3 * margin :] = signal_ref[:, head * band : (head + 1) * band].astype(F32)

    columns = picks.shape[2]
    size = first_ref.shape[2]
    sub = columns // groups
    parts = groups // sub
    part_heads = heads // parts
    deep = part_heads * band
    total_lanes = freq_count * columns
    channel = shuffle_ref.shape[1]
    spread = jnp.where(
        lax.broadcasted_iota(jnp.int32, (channel, total_lanes), 1) // sub
        == lax.broadcasted_iota(jnp.int32, (channel, total_lanes), 0),
        1.0,
        0.0,
    ).astype(BF16)
    taken = jnp.broadcast_to(shuffle_ref[...].astype(F32), (16, channel)).astype(BF16)
    lane = lax.broadcasted_iota(jnp.int32, (16, total_lanes), 1)
    taken = ordered_dot(taken, spread) + (lane % sub * size).astype(F32)
    row_ids = lax.broadcasted_iota(jnp.int32, (deep, columns), 0).astype(F32)
    for target in range(freq_count):
        source = taken[0:1, target * columns : (target + 1) * columns]
        picks[target] = jnp.where(row_ids == source, 1.0, 0.0).astype(BF16)
    pl.semaphore_wait(barrier, freq_count + tm_count - 2)

    def halo_copy():
        return pltpu.make_async_remote_copy(
            src_ref=signal_ref.at[pl.ds(count - 2 * margin, 2 * margin)],
            dst_ref=halo,
            send_sem=halo_sem.at[0],
            recv_sem=halo_sem.at[1],
            device_id={"tm": lax.rem(at_tm + 1, tm_count)},
            device_id_type=MESH,
        )

    @pl.when(at_tm < tm_count - 1)
    def _():
        halo_copy().start()

    def marks_copy(source, target):
        return pltpu.make_async_remote_copy(
            src_ref=marks_ref,
            dst_ref=marks.at[source],
            send_sem=b_send.at[target],
            recv_sem=b_recv.at[source],
            device_id={"tm": target},
            device_id_type=MESH,
        )

    for step in range(1, tm_count):
        marks_copy(at_tm, lax.rem(at_tm + step, tm_count)).start()
    marks[at_tm] = marks_ref[...]
    loads[0].wait()
    for load in loads[1:]:
        load.start()
    spread_weights(first_ref, spread_first)

    @pl.when(at_tm > 0)
    def _():
        halo_copy().wait_recv()
        for head in range(heads):
            padded[head, margin : 3 * margin] = halo[:, head * band : (head + 1) * band].astype(F32)

    def convolve(source, head, top, length, spread_ref):
        windows = [source[head, top - tap : top - tap + length] for tap in range(taps)]
        windows = jnp.concatenate([window.astype(BF16) for window in windows], axis=1)
        return ordered_dot(windows, spread_ref[head].reshape(taps * band, band))

    cuts = [(0, 2 * margin + part)] + [
        (2 * margin + i * part, part) for i in range(1, splits)
    ]

    def z_copy(source, target, half):
        top, length = cuts[half]
        return pltpu.make_async_remote_copy(
            src_ref=sending.at[target, pl.ds(top, length)],
            dst_ref=arrived.at[source, pl.ds(top, length)],
            send_sem=z_send.at[target * splits + half],
            recv_sem=z_recv.at[source * splits + half],
            device_id={"freq": target},
            device_id_type=MESH,
        )

    def shuffle_for(target, half, out):
        top, length = cuts[half]
        for piece in range(parts):
            held = [
                first[piece * part_heads + i, top : top + length] for i in range(part_heads)
            ]
            out[target, top : top + length, piece * columns : (piece + 1) * columns] = ordered_dot(
                jnp.concatenate(held, axis=1), picks[target]
            ).astype(BF16)

    def partner(step):
        chips = freq_count // 2
        chip = lax.rem(at_freq // 2 + step // 2 + 1, chips)
        return chip * 2 + lax.rem(at_freq % 2 + 1 + step % 2, 2)

    for half in range(splits):
        top, length = cuts[half]

        def convolve_first(head, carry):
            total = convolve(padded, head, margin + top, length, spread_first)
            first[head, top : top + length] = (total / (1.0 + jnp.exp(-total))).astype(BF16)
            return carry

        lax.fori_loop(0, heads, convolve_first, 0)

        def shuffle_step(step, carry):
            target = partner(step)
            shuffle_for(target, half, sending)
            z_copy(at_freq, target, half).start()
            return carry

        lax.fori_loop(0, freq_count - 1, shuffle_step, 0)
    for half in range(splits):
        shuffle_for(at_freq, half, arrived)
    for load in loads[1:]:
        load.wait()
    spread_weights(second_ref, spread_second)

    per_band = groups // heads
    chunk = per_band * sub
    lane_from = lax.broadcasted_iota(jnp.int32, (band, band), 0)
    lane_to = lax.broadcasted_iota(jnp.int32, (band, band), 1)
    wanted = (lane_from % chunk) // sub * size + lane_from // chunk * sub + lane_from % sub
    regroup = jnp.where(wanted == lane_to, 1.0, 0.0).astype(BF16)

    def regroup_half(half):
        top, length = cuts[half]
        for step in range(freq_count - 1):
            z_copy(partner(step), at_freq, half).wait_recv()
        for head in range(heads):
            pieces = [
                arrived[
                    source,
                    top : top + length,
                    piece * columns + head * chunk : piece * columns + (head + 1) * chunk,
                ]
                for source in range(freq_count)
                for piece in range(parts)
            ]
            shuffled[head, top : top + length] = ordered_dot(
                jnp.concatenate(pieces, axis=1), regroup
            )

    own_head, own_split = at_tm // splits, at_tm % splits

    def pair_copy(source, head, half):
        return pltpu.make_async_remote_copy(
            src_ref=pair_out.at[head, pl.ds(half * part, part)],
            dst_ref=pairs.at[source, pl.ds(half * part, part)],
            send_sem=kv_send.at[head * splits + half],
            recv_sem=kv_recv.at[source * splits + half],
            device_id={"tm": head * splits + own_split},
            device_id_type=MESH,
        )

    def forward_copy(source, step, half):
        return pltpu.make_async_remote_copy(
            src_ref=pairs.at[source, pl.ds(half * part, part)],
            dst_ref=pairs.at[source, pl.ds(half * part, part)],
            send_sem=forward_send.at[(source * splits + step) * splits + half],
            recv_sem=kv_recv.at[source * splits + half],
            device_id={"tm": own_head * splits + lax.rem(own_split + step, splits)},
            device_id_type=MESH,
        )

    def forward(source, half):
        for step in range(1, splits):
            forward_copy(source, step, half).start()

    def query_copy(source, head, split):
        target = head * splits + split
        return pltpu.make_async_remote_copy(
            src_ref=query_out.at[target],
            dst_ref=queries.at[source],
            send_sem=q_send.at[target],
            recv_sem=q_recv.at[source],
            device_id={"tm": target},
            device_id_type=MESH,
        )

    def project(head, half):
        top = half * part
        total = padded[head, 3 * margin + top : 3 * margin + top + part]
        total = total + convolve(shuffled, head, 2 * margin + top, part, spread_second)
        rounded = total.astype(BF16)
        resid[head, top : top + part] = rounded
        pair_out[head, top : top + part, 0:head_size] = ordered_dot(
            rounded, wk_ref[head]
        ).astype(BF16)
        pair_out[head, top : top + part, head_size:] = ordered_dot(
            rounded, wv_ref[head]
        ).astype(BF16)
        query_out[head * splits + half] = ordered_dot(rounded, wq_ref[head]).astype(BF16)

    for half in range(splits):
        regroup_half(half)

        def project_step(step, carry):
            head = lax.rem(own_head + step, heads)
            project(head, half)
            pair_copy(at_tm, head, half).start()
            query_copy(at_tm, head, half).start()
            return carry

        lax.fori_loop(1, heads, project_step, 0)
        project(own_head, half)
        top = half * part
        pairs[at_tm, top : top + part] = pair_out[own_head, top : top + part]
        forward(at_tm, half)

        @pl.when(own_split != half)
        def _():
            query_copy(at_tm, own_head, half).start()

    queries[at_tm] = query_out[at_tm]

    def att_copy(source, target):
        return pltpu.make_async_remote_copy(
            src_ref=att_out.at[target],
            dst_ref=att_in.at[source],
            send_sem=a_send.at[target],
            recv_sem=a_recv.at[source],
            device_id={"tm": target},
            device_id_type=MESH,
        )

    def await_source(source):
        @pl.when(at_tm != source)
        def _():
            marks_copy(source, at_tm).wait_recv()
            query_copy(source, own_head, own_split).wait_recv()

        @pl.when(own_split != source % splits)
        def _():
            for half in range(splits):
                pair_copy(source, own_head, half).wait_recv()

    factor = math.log2(math.e) / math.sqrt(head_size)
    ahead = -(-BLOCK_MOST // LANES) * LANES
    contract = (((1,), (1,)), ((), ()))
    for half in range(splits):
        for step in range(1, heads):
            source = lax.rem(own_head + heads - step, heads) * splits + own_split
            pair_copy(source, own_head, half).wait_recv()
            forward(source, half)
    await_source(0)
    for block in range(tm_count):
        if block + 1 < tm_count:
            await_source(block + 1)
        asked = queries[block]
        near = pairs[block]
        near_marks = marks[block][0:1].astype(F32)
        if block + 1 < tm_count:
            near = jnp.concatenate([near, pairs[block + 1, 0:ahead]], axis=0)
            near_marks = jnp.concatenate(
                [near_marks, marks[block + 1][0:1, 0:ahead].astype(F32)], axis=1
            )
        offset = pl.multiple_of(own_split * part, LANES)
        mine = marks[block, 0:1, pl.ds(offset, part)].astype(F32)
        mine = jnp.transpose(jnp.broadcast_to(mine, (part, part)))[:, 0:1]
        near_scores = lax.dot_general(
            asked, near[:, 0:head_size], contract, preferred_element_type=F32
        )
        near_scores = jnp.where(near_marks <= mine, near_scores, -1e30)
        peak = jnp.max(near_scores, axis=1, keepdims=True)
        if block > 0:
            far = pairs[0:block].reshape(block * count, 2 * head_size)
            far_scores = lax.dot_general(
                asked, far[:, 0:head_size], contract, preferred_element_type=F32
            )
            peak = jnp.maximum(peak, jnp.max(far_scores, axis=1, keepdims=True))
        weights = jnp.exp2((near_scores - peak) * factor)
        total = jnp.sum(weights, axis=1, keepdims=True)
        summed = ordered_dot(weights.astype(BF16), near[:, head_size:])
        if block > 0:
            weights = jnp.exp2((far_scores - peak) * factor)
            total = total + jnp.sum(weights, axis=1, keepdims=True)
            summed = summed + ordered_dot(weights.astype(BF16), far[:, head_size:])
        att_out[block] = (summed / total).astype(BF16)

        @pl.when(at_tm != block)
        def _():
            att_copy(at_tm, block).start()

    att_in[at_tm] = att_out[at_tm]
    for source in range(tm_count):

        @pl.when(at_tm != source)
        def _():
            att_copy(source, at_tm).wait_recv()

        head, split = source // splits, source % splits
        top = split * part
        added = ordered_dot(att_in[source], wo_ref[head])
        out_ref[top : top + part, head * band : (head + 1) * band] = (
            resid[head, top : top + part].astype(F32) + added
        ).astype(BF16)

    @pl.when(at_tm < tm_count - 1)
    def _():
        halo_copy().wait_send()

    for half in range(splits):
        for step in range(freq_count - 1):
            z_copy(at_freq, partner(step), half).wait_send()
        for step in range(1, heads):
            pair_copy(at_tm, lax.rem(own_head + step, heads), half).wait_send()
        for head in range(heads):
            for step in range(1, splits):
                forward_copy(head * splits + own_split, step, half).wait_send()
    for step in range(1, tm_count):
        target = lax.rem(at_tm + step, tm_count)
        marks_copy(at_tm, target).wait_send()
        query_copy(at_tm, target // splits, target % splits).wait_send()
        att_copy(at_tm, target).wait_send()


def per_device_fused(
    signal,
    conv_first,
    conv_second,
    shuffle,
    blocks,
    query_weight,
    key_weight,
    value_weight,
    out_weight,
):
    freq_count, tm_count = lax.axis_size("freq"), lax.axis_size("tm")
    count, width = signal.shape
    groups, taps, size, _ = conv_first.shape
    heads, band, head_size = query_weight.shape
    margin = taps - 1
    rows = count + 2 * margin
    part = count * heads // tm_count
    splits = tm_count // heads
    columns = groups * groups
    deep = heads * band * LANES // columns
    vmem = pl.BlockSpec(memory_space=pltpu.VMEM)
    hbm = pl.BlockSpec(memory_space=pl.ANY)
    dma = pltpu.SemaphoreType.DMA
    return pl.pallas_call(
        functools.partial(layer_kernel, freq_count, tm_count),
        out_shape=jax.ShapeDtypeStruct((count, width), BF16),
        in_specs=[vmem] * 3 + [hbm] * 6,
        out_specs=vmem,
        scratch_shapes=[
            pltpu.VMEM(conv_first.shape, BF16),
            pltpu.VMEM(conv_second.shape, BF16),
            pltpu.VMEM(query_weight.shape, BF16),
            pltpu.VMEM(key_weight.shape, BF16),
            pltpu.VMEM(value_weight.shape, BF16),
            pltpu.VMEM(out_weight.shape, BF16),
            pltpu.VMEM((freq_count, deep, LANES), BF16),
            pltpu.VMEM((8, count), jnp.int32),
            pltpu.VMEM((heads, rows + margin, band), F32),
            pltpu.VMEM((heads, taps, band, band), BF16),
            pltpu.VMEM((heads, taps, band, band), BF16),
            pltpu.VMEM((2 * margin, width), BF16),
            pltpu.VMEM((heads, rows, band), BF16),
            pltpu.VMEM((freq_count, rows, columns), BF16),
            pltpu.VMEM((freq_count, rows, columns), BF16),
            pltpu.VMEM((heads, rows, band), F32),
            pltpu.VMEM((heads, count, band), BF16),
            pltpu.VMEM((heads, count, 2 * head_size), BF16),
            pltpu.VMEM((tm_count, part, head_size), BF16),
            pltpu.VMEM((tm_count, count, 2 * head_size), BF16),
            pltpu.VMEM((tm_count, part, head_size), BF16),
            pltpu.VMEM((tm_count, 8, count), jnp.int32),
            pltpu.VMEM((tm_count, part, head_size), BF16),
            pltpu.VMEM((tm_count, part, head_size), BF16),
            dma((2,)),
            dma((freq_count * splits,)),
            dma((freq_count * splits,)),
        ]
        + [dma((tm_count,))] * 2
        + [dma((tm_count,)), dma((tm_count * splits,))]
        + [dma((tm_count,))] * 4
        + [dma((tm_count * splits * splits,)), dma((6,))],
        compiler_params=pltpu.CompilerParams(
            collective_id=0, has_side_effects=True, vmem_limit_bytes=56 * 1024 * 1024
        ),
        cost_estimate=pl.CostEstimate(
            flops=10**10, bytes_accessed=8 * 10**6, transcendentals=2 * 10**6
        ),
    )(
        signal,
        shuffle[None, :],
        blocks[None, :],
        conv_first,
        conv_second,
        query_weight,
        key_weight,
        value_weight,
        out_weight,
    )


def fits_fused(signal, conv_first, query_weight):
    tm_count = lax.axis_size("tm")
    count = signal.shape[0]
    groups, taps, size, _ = conv_first.shape
    heads, band, head_size = query_weight.shape
    return (
        tm_count % heads == 0
        and (count * heads) % (LANES * tm_count) == 0
        and (groups * groups) % LANES == 0
        and LANES % groups == 0
        and heads % (groups * groups // LANES) == 0
        and lax.axis_size("freq") % 2 == 0
        and groups % heads == 0
        and heads * band == signal.shape[1]
        and (taps - 1) % 8 == 0
        and LANES % size == 0
        and band % LANES == 0
        and head_size % LANES == 0
        and size % 16 == 0
    )


def passed_along(block, axis, distance):
    devices = range(lax.axis_size(axis))
    route = [(i - distance, i) for i in devices if i - distance in devices]
    return lax.ppermute(block, axis, route)


def conv_local(padded, weights, length, form):
    margin = weights.shape[1] - 1
    result = None
    for offset in range(weights.shape[1]):
        term = jnp.einsum(
            form,
            padded[margin - offset : margin - offset + length],
            weights[:, offset],
            preferred_element_type=jnp.float32,
        )
        result = term if result is None else result + term
    return result


def split_range(count, width):
    return [(offset, min(offset + width, count)) for offset in range(0, count, width)]


def update_tile(state, query_part, query_marks, key_part, value_part, key_marks):
    peak, total, summed = state
    scale = 1.0 / math.sqrt(query_part.shape[2])
    scores = (
        jnp.einsum("qhd,khd->hqk", query_part, key_part, preferred_element_type=jnp.float32) * scale
    )
    seen = key_marks[None, None, :] <= query_marks[None, :, None]
    masked = jnp.where(seen, scores, jnp.float32(-1e30))
    new_peak = jnp.maximum(peak, jnp.max(masked, axis=2))
    weights = jnp.where(seen, jnp.exp(masked - new_peak[:, :, None]), jnp.float32(0.0))
    factor = jnp.exp(peak - new_peak)
    total = total * factor + jnp.sum(weights, axis=2)
    summed = summed * factor[:, :, None] + jnp.einsum(
        "hqk,khd->hqd", weights.astype(jnp.bfloat16), value_part, preferred_element_type=jnp.float32
    )
    return (new_peak, total, summed)


def unchanged(state, *others):
    return state


def make_fold(queries, query_marks):
    count = queries.shape[0]
    query_cuts = split_range(count, max(1, count // 2))

    def fold(carry, piece, start):
        key_rows, value_rows, key_marks = piece
        key_cuts = split_range(key_rows.shape[0], max(1, count // 2))
        peak, total, summed = carry
        results = []
        for top_row, end_row in query_cuts:
            state = (
                peak[:, top_row:end_row],
                total[:, top_row:end_row],
                summed[:, top_row:end_row],
            )
            for key_top, key_end in key_cuts:
                needed = jnp.min(key_marks[key_top:key_end]) <= jnp.max(
                    query_marks[top_row:end_row]
                )
                state = lax.cond(
                    needed,
                    update_tile,
                    unchanged,
                    state,
                    queries[top_row:end_row],
                    query_marks[top_row:end_row],
                    key_rows[key_top:key_end],
                    value_rows[key_top:key_end],
                    key_marks[key_top:key_end],
                )
            results.append(state)
        return tuple(
            (jnp.concatenate([entry[member] for entry in results], axis=1) for member in range(3))
        )

    return fold


def start_state(heads_here, count, head_size):
    return (
        jnp.full((heads_here, count), -1e30, jnp.float32),
        jnp.zeros((heads_here, count), jnp.float32),
        jnp.zeros((heads_here, count, head_size), jnp.float32),
    )


def finish(state):
    peak, total, summed = state
    return jnp.transpose(summed / total[:, :, None], (1, 0, 2)).astype(jnp.bfloat16)


def per_device_plain(
    signal,
    conv_first,
    conv_second,
    shuffle,
    blocks,
    query_weight,
    key_weight,
    value_weight,
    out_weight,
):
    count, width = signal.shape
    groups_here = conv_first.shape[0]
    group_size = conv_first.shape[2]
    margin = conv_first.shape[1] - 1
    local = signal.reshape(count, groups_here, group_size)
    selector = (shuffle[None, :] == jnp.arange(group_size, dtype=jnp.int32)[:, None]).astype(
        jnp.bfloat16
    )
    before = passed_along(local[count - 2 * margin :], "tm", 1)
    padded = jnp.concatenate([before, local], axis=0)
    first = jax.nn.silu(conv_local(padded, conv_first, count + margin, "tgi,gio->tgo")).astype(
        jnp.bfloat16
    )
    permuted = jnp.einsum(
        "tgj,jk->tgk", first, selector, preferred_element_type=jnp.float32
    ).astype(jnp.bfloat16)
    shuffled = lax.all_to_all(permuted, "freq", split_axis=2, concat_axis=1, tiled=True)
    second = conv_local(shuffled, conv_second, count, "tgk,kgo->tko")
    resid = (signal.astype(jnp.float32) + second.reshape(count, width)).astype(jnp.bfloat16)
    heads_here, band, head_size = query_weight.shape
    bands = resid.reshape(count, heads_here, band)
    queries = jnp.einsum(
        "thc,hcd->thd", bands, query_weight, preferred_element_type=jnp.float32
    ).astype(jnp.bfloat16)
    keys = jnp.einsum("thc,hcd->thd", bands, key_weight, preferred_element_type=jnp.float32).astype(
        jnp.bfloat16
    )
    values = jnp.einsum(
        "thc,hcd->thd", bands, value_weight, preferred_element_type=jnp.float32
    ).astype(jnp.bfloat16)
    initial = start_state(heads_here, count, head_size)
    fold = make_fold(queries, blocks)
    state = fold(
        initial,
        (
            lax.all_gather(keys, "tm", axis=0, tiled=True),
            lax.all_gather(values, "tm", axis=0, tiled=True),
            lax.all_gather(blocks, "tm", axis=0, tiled=True),
        ),
        jnp.int32(0),
    )
    attended = finish(state)
    added = jnp.einsum("thd,hdc->thc", attended, out_weight, preferred_element_type=jnp.float32)
    return (resid.astype(jnp.float32) + added.reshape(count, width)).astype(jnp.bfloat16)


def per_device(*args):
    if fits_fused(args[0], args[1], args[5]):
        return per_device_fused(*args)
    return per_device_plain(*args)


def solution(mesh):
    in_specs = (
        P("tm", "freq"),
        P("freq", None, None, None),
        P("freq", None, None, None),
        P(),
        P("tm"),
        P("freq", None, None),
        P("freq", None, None),
        P("freq", None, None),
        P("freq", None, None),
    )
    out_specs = P("tm", "freq")
    return jax.shard_map(
        per_device, mesh=mesh, in_specs=in_specs, out_specs=out_specs, check_vma=False
    )
```
